32 devices in a mesh: fsdp: 4 (over x, core), expert: 8 (over z, y).
Axes of the slice: x: 2, y: 2, z: 4, core: 2. Of those that a mesh axis runs over, the one named last changes fastest.
Arguments:
- tokens: bfloat16 [4096, 768], P(('fsdp', 'expert')), may hold values from -6 to 6
- cotangent: bfloat16 [4096, 768], P(('fsdp', 'expert')), may hold values from -6 to 6
- project_in: bfloat16 [768, 2304], P(('fsdp', 'expert')), may hold values from -0.21875 to 0.21875
- project_out: bfloat16 [768, 768], P(('fsdp', 'expert')), may hold values from -0.875 to 0.875
- router: bfloat16 [768, 8], P(('fsdp', 'expert')), may hold values from -0.14941406 to 0.14941406
- first_gain: bfloat16 [768], P(('fsdp', 'expert')), may hold values from 0.5 to 1.5
- second_gain: bfloat16 [768], P(('fsdp', 'expert')), may hold values from 0.5 to 1.5
- bias_table: float32 [32, 12], replicated, may hold values from -4 to 4
- expert_up: bfloat16 [8, 768, 3072], P('expert', None, 'fsdp'), may hold values from -0.21875 to 0.21875
- expert_down: bfloat16 [8, 3072, 768], P('expert', 'fsdp'), may hold values from -0.109375 to 0.109375
- positions: int32 [4096], P(('fsdp', 'expert')), may hold values from 0 to 127, as said below
- buckets: int32 [128], replicated, may hold values from 0 to 31, as said below
- routes: int32 [4096, 2], P(('fsdp', 'expert')), may hold values from 0 to 7, as said below
- slots: int32 [4096, 2], P(('fsdp', 'expert')), may hold values from 0 to 47, as said below
Outputs:
- mixed: bfloat16 [4096, 768], P(('fsdp', 'expert'))
- grad_tokens: bfloat16 [4096, 768], P(('fsdp', 'expert'))
- grad_project_in: float32 [768, 2304], P(('fsdp', 'expert'))
- grad_project_out: float32 [768, 768], P(('fsdp', 'expert'))
- grad_router: float32 [768, 8], P(('fsdp', 'expert'))
- grad_first_gain: float32 [768], P(('fsdp', 'expert'))
- grad_second_gain: float32 [768], P(('fsdp', 'expert'))
- grad_bias_table: float32 [32, 12], replicated
- grad_expert_up: float32 [8, 768, 3072], P('expert', None, 'fsdp')
- grad_expert_down: float32 [8, 3072, 768], P('expert', 'fsdp')
The draws below stay inside these ranges and needn't reach their ends.
Inputs may be any that keep to these rules, and one draw needn't show every extreme that they name: `positions`: each device's tokens hold whole sequences in order: a position is 0 at a sequence's first token and rises by one along it. `buckets`: 0 at distance 0, never falling with the distance. `routes`: the two experts of a token differ; the tokens of one device name no expert more than 48 times. routes of one device to one expert have different slots.
All inputs are finite; a program needn't handle non-finite values.
Results may differ from the reference program's by a relative error of at most 0.015.
Values may be sent and summed in bfloat16 or wider, within the bound.
No kernel may reach another device: no remote copies, remote signals or barrier semaphores. Data moves between devices by JAX's collectives and lax.ppermute only.
A program may use at most 128 MiB of HBM per device.

```python
import jax
import jax.numpy as jnp
from jax import lax

D = 768
HEADS = 12
HEAD = 64
FF = 3072
BUCKETS = 32
TOK_DEV = 128
EXPERTS = 8
CAP = 48
TOKENS = 4096
DEVICES = 32


def route_layout(key):
    half = EXPERTS // 2
    pair_count = half * CAP

    def one_device(device_key, starred):
        keys = jax.random.split(device_key, CAP + 3)
        orders = jax.vmap(lambda row_key: jax.random.permutation(row_key, EXPERTS))(keys[:CAP])
        lefts = orders[:, :half].reshape(-1)
        rights = orders[:, half:].reshape(-1)
        slot_of = jnp.repeat(jnp.arange(CAP, dtype=jnp.int32), half)
        marked = (lefts == starred) | (rights == starred)
        noise = jax.random.randint(keys[CAP], (pair_count,), 0, 1 << 20) * pair_count + jnp.arange(pair_count, dtype=jnp.int32)
        ranking = jnp.where(marked, -1, noise)
        picked = jnp.argsort(ranking, stable=True)[:TOK_DEV]
        picked = picked[jax.random.permutation(keys[CAP + 1], TOK_DEV)]
        flipped = jax.random.randint(keys[CAP + 2], (TOK_DEV,), 0, 2) == 1
        primary = jnp.where(flipped, rights[picked], lefts[picked])
        secondary = jnp.where(flipped, lefts[picked], rights[picked])
        slot_pair = jnp.stack([slot_of[picked], slot_of[picked]], axis=1)
        return (jnp.stack([primary, secondary], axis=1), slot_pair)
    device_keys = jax.random.split(key, DEVICES + 1)
    starred_rows = jax.random.randint(device_keys[DEVICES], (DEVICES // EXPERTS,), 0, EXPERTS)
    starred_all = jnp.repeat(starred_rows, EXPERTS)
    route_table, slot_table = jax.vmap(one_device)(device_keys[:DEVICES], starred_all)
    return (route_table.reshape(-1, 2).astype(jnp.int32), slot_table.reshape(-1, 2).astype(jnp.int32))


def draw_routes(key, part):
    shared = route_layout(key)
    return shared[0]


def draw_slots(key, part):
    shared = route_layout(key)
    return shared[1]


def draw_positions(key, part):
    key = jax.random.fold_in(key, 11)
    first_key, second_key = jax.random.split(key)
    starts = jax.random.randint(first_key, (DEVICES, TOK_DEV), 0, 32) == 0
    column = jnp.arange(TOK_DEV, dtype=jnp.int32)
    single = jax.random.randint(second_key, (), 0, DEVICES)
    row_index = jnp.arange(DEVICES, dtype=jnp.int32)[:, None]
    starts = jnp.where(row_index == single, False, starts)
    starts = starts | (column[None, :] == 0)
    last_start = lax.cummax(jnp.where(starts, column[None, :], 0), axis=1)
    return (column[None, :] - last_start).reshape(-1).astype(jnp.int32)


def draw_buckets(key, part):
    key = jax.random.fold_in(key, 12)
    distance = jnp.arange(TOK_DEV, dtype=jnp.int32)
    rising = (jax.random.randint(key, (TOK_DEV,), 0, 4) == 0).astype(jnp.int32)
    rising = jnp.where(distance < 8, 1, rising)
    rising = jnp.where(distance == 0, 0, rising)
    levels = jnp.minimum(jnp.cumsum(rising), BUCKETS - 1)
    return jnp.where(distance == TOK_DEV - 1, BUCKETS - 1, levels).astype(jnp.int32)


def steps_of(key, extent, cuts, least, high):
    factor_of = 1.0
    for dim, blocks in cuts:
        steps = jax.random.uniform(jax.random.fold_in(jax.random.fold_in(key, 6), dim), (blocks,), jnp.float32, least / len(cuts), high / len(cuts))
        factor_of = factor_of * jnp.repeat(jnp.exp(steps), extent[dim] // blocks).reshape((-1,) + (1,) * (len(extent) - 1 - dim))
    return factor_of


def scatter_about(stream_key, shape, width, reach, cuts=(), kind=jnp.bfloat16):
    loudness = steps_of(stream_key, shape, cuts, -0.22, 0.18) if cuts else 1.0
    entries = jax.random.normal(stream_key, shape, jnp.float32) * width * loudness
    return jnp.minimum(jnp.maximum(entries, -reach), reach).astype(kind)


def setup_inputs(seed: int = 0) -> dict:
    arg_keys = jax.random.split(jax.random.key(seed), 15)
    tokens = scatter_about(arg_keys[0], (TOKENS, D), 1.0, 6.0, ((0, 32),))
    cotangent = scatter_about(arg_keys[1], (TOKENS, D), 1.0, 6.0, ((0, 32),))
    project_in = scatter_about(arg_keys[2], (D, 3 * D), D ** -0.5, 0.21875, ((0, 32),))
    project_out = scatter_about(arg_keys[3], (D, D), (D // 16) ** -0.5, 0.875, ((0, 32),))
    router = scatter_about(arg_keys[4], (D, EXPERTS), 0.025, 0.14941406, ((0, 32),))
    first_gain = jnp.clip(1.0 + 0.1 * jax.random.normal(arg_keys[5], (D,), jnp.float32), 0.5, 1.5).astype(jnp.bfloat16)
    second_gain = jnp.clip(1.0 + 0.1 * jax.random.normal(arg_keys[6], (D,), jnp.float32), 0.5, 1.5).astype(jnp.bfloat16)
    bias_table = scatter_about(arg_keys[7], (BUCKETS, HEADS), 1.0, 4.0, (), jnp.float32)
    expert_up = scatter_about(arg_keys[8], (EXPERTS, D, FF), D ** -0.5, 0.21875, ((0, 8), (2, 4)))
    expert_down = scatter_about(arg_keys[9], (EXPERTS, FF, D), FF ** -0.5, 0.109375, ((0, 8), (1, 4)))
    positions = draw_positions(jax.random.fold_in(arg_keys[14], 71), 0)
    buckets = draw_buckets(jax.random.fold_in(arg_keys[14], 71), 0)
    routes = draw_routes(jax.random.fold_in(arg_keys[14], 71), 0)
    slots = draw_slots(jax.random.fold_in(arg_keys[14], 71), 0)
    return dict(tokens=tokens, cotangent=cotangent, project_in=project_in, project_out=project_out, router=router, first_gain=first_gain, second_gain=second_gain, bias_table=bias_table, expert_up=expert_up, expert_down=expert_down, positions=positions, buckets=buckets, routes=routes, slots=slots)


@jax.custom_vjp
def low(v):
    return lax.optimization_barrier(v.astype(jnp.bfloat16)).astype(jnp.float32)

@jax.custom_vjp
def low_back(v):
    return v

def low_keep(v):
    return (low(v), None)

def low_pass(kept, grad):
    return (grad,)

def back_keep(v):
    return (v, None)

def back_low(kept, grad):
    return (low(grad),)
low.defvjp(low_keep, low_pass)
low_back.defvjp(back_keep, back_low)

def rms_scale(value, gain):
    return value * lax.rsqrt(lax.optimization_barrier(jnp.mean(value * value, axis=-1, keepdims=True)) + 1e-06) * gain

def reference(tokens, cotangent, project_in, project_out, router, first_gain, second_gain, bias_table, expert_up, expert_down, positions, buckets, routes, slots):
    highest = lax.Precision.HIGHEST
    places = jnp.arange(TOK_DEV).astype(jnp.int32)
    distance = places[:, None] - places[None, :]
    bucket_pair = jnp.take(buckets, jnp.clip(distance, 0, TOK_DEV - 1).astype(jnp.int32))
    device = (jnp.arange(TOKENS) // TOK_DEV).astype(jnp.int32)
    target = (routes * (DEVICES * CAP) + device[:, None] * CAP + slots).astype(jnp.int32)
    flat = target.reshape(-1)

    def device_attention(items):
        query, keys, values, place, table = items
        raw = low_back(jnp.einsum('qhd,khd->hqk', query, keys, precision=highest))
        bias = jnp.transpose(table[bucket_pair], (2, 0, 1))
        valid = (distance >= 0) & (distance <= place[:, None])
        scores = jnp.where(valid[None], raw * 0.125 + bias, -1e+30)
        top = lax.optimization_barrier(jnp.max(scores, axis=-1, keepdims=True))
        expo = jnp.exp(scores - top)
        probs = low(expo / lax.optimization_barrier(jnp.sum(expo, axis=-1, keepdims=True)))
        return jnp.einsum('hqk,khd->qhd', probs, values, precision=highest)

    def one_expert(items):
        rows, weight_up, weight_down = items
        inner = low_back(jnp.dot(rows, weight_up, precision=highest))
        activated = low(jax.nn.gelu(inner))
        return jnp.dot(activated, weight_down, precision=highest)

    def forward(inputs, weight_in, weight_out, router_matrix, gain_one, gain_two, table, weight_up, weight_down):
        normed = low(rms_scale(inputs, gain_one))
        joint = low(low_back(jnp.dot(normed, weight_in, precision=highest)))
        grouped = joint.reshape(DEVICES, TOK_DEV, 3, HEADS, HEAD)
        tables = jnp.broadcast_to(table, (DEVICES, BUCKETS, HEADS))
        attended = lax.map(jax.checkpoint(device_attention), (grouped[:, :, 0], grouped[:, :, 1], grouped[:, :, 2], positions.reshape(DEVICES, TOK_DEV), tables))
        attended = low(low_back(attended.reshape(TOKENS, D)))
        first = inputs + low_back(jnp.dot(attended, weight_out, precision=highest))
        second = low(rms_scale(first, gain_two))
        logits = low_back(jnp.dot(second, router_matrix, precision=highest))
        chosen = jnp.take_along_axis(logits, routes, axis=1)
        gates = jax.nn.softmax(chosen, axis=1)
        buffer = jnp.zeros((EXPERTS * DEVICES * CAP, D), jnp.float32).at[flat].set(jnp.repeat(second, 2, axis=0))
        buffer = low_back(buffer).reshape(EXPERTS, DEVICES * CAP, D)
        results = lax.map(jax.checkpoint(one_expert), (buffer, weight_up, weight_down))
        results = low(low_back(results)).reshape(EXPERTS * DEVICES * CAP, D)
        picked = results[flat].reshape(TOKENS, 2, D)
        return first + lax.optimization_barrier(jnp.sum(gates[:, :, None] * picked, axis=1))
    floats = (tokens.astype(jnp.float32), project_in.astype(jnp.float32), project_out.astype(jnp.float32), router.astype(jnp.float32), first_gain.astype(jnp.float32), second_gain.astype(jnp.float32), bias_table.astype(jnp.float32), expert_up.astype(jnp.float32), expert_down.astype(jnp.float32))
    output, pullback = jax.vjp(forward, *floats)
    grads = pullback(cotangent.astype(jnp.float32))
    return (output.astype(jnp.bfloat16), grads[0].astype(jnp.bfloat16), grads[1], grads[2], grads[3], grads[4], grads[5], grads[6], grads[7], grads[8])
```

```python
import jax
import jax.numpy as jnp
from jax import lax
from jax.sharding import PartitionSpec as P

HEADS = 12
HEAD = 64
BUCKETS = 32
LANES = 128
BF = jnp.bfloat16
F32 = jnp.float32


def rms_scale(value, gain):
    return value * lax.rsqrt(jnp.mean(value * value, axis=-1, keepdims=True) + 1e-06) * gain


def contract_rows(left, right):
    return lax.dot_general(left, right, (((0,), (0,)), ((), ())), preferred_element_type=F32)


def contract_cols(left, right):
    return lax.dot_general(left, right, (((1,), (1,)), ((), ())), preferred_element_type=F32)


def matmul(left, right):
    return jnp.dot(left, right, preferred_element_type=F32)


def swap(value, step):
    axis, bit = step
    size = lax.axis_size(axis)
    return lax.ppermute(value, axis, [(i, i ^ bit) for i in range(size)])


def bits_of(axis):
    size = lax.axis_size(axis)
    bits = []
    while size > 1:
        size //= 2
        bits.append((axis, size))
    return bits


def canonical():
    return bits_of("fsdp") + bits_of("expert")


def split_at(shape, dims, place):
    before = 1
    for n in dims[:place]:
        before *= n
    after = shape[0]
    for n in dims[place + 1 :]:
        after *= n
    return before, after


def grow(own, other, rows, dims, place):
    before, after = split_at((rows,), dims, place)
    width = own.shape[-1]
    parts = [own.reshape(before, 1, after, width), other.reshape(before, 1, after, width)]
    dims[place] = 2
    return jnp.concatenate(parts, axis=1).reshape(2 * before * after, width)


def gather_blocks(value, order):
    names = canonical()
    rows = value.shape[0]
    dims = [1] * len(names)
    held = value
    for step in order[:-2]:
        held = grow(held, swap(held, step), rows, dims, names.index(step))
    last, core = order[-2:]
    near = swap(held, last)
    held_core = swap(held, core)
    near_core = swap(near, core)
    copy = list(dims)
    place = names.index(last)
    mine = grow(held, near, rows, dims, place)
    theirs = grow(held_core, near_core, rows, copy, place)
    return grow(mine, theirs, rows, dims, names.index(core))


def scatter_blocks(value, order):
    names = canonical()
    dims = [2] * len(names)
    rows = value.shape[0]
    for _ in names:
        rows //= 2
    held = value
    for number, step in enumerate(order):
        place = names.index(step)
        before, after = split_at((rows,), dims, place)
        width = held.shape[-1]
        view = held.reshape(before, 2, after, width)
        arrived = swap(view[:, 1], step)
        total = view[:, 0].astype(F32) + arrived.astype(F32)
        dims[place] = 1
        held = total.reshape(before * after, width)
        if number < len(order) - 1:
            held = held.astype(BF)
    return held


def total_over_all(value):
    for step in canonical():
        value = value + swap(value, step)
    return value


def exchange(value):
    experts = lax.axis_size("expert")
    shape = value.shape
    blocks = value.reshape((experts, shape[0] // experts) + shape[1:])
    return lax.all_to_all(blocks, "expert", split_axis=0, concat_axis=0, tiled=True).reshape(shape)


def spread(value):
    held = [value]
    for step in reversed(bits_of("fsdp")[:-1]):
        held = held + [swap(part, step) for part in held]
    core = bits_of("fsdp")[-1]
    return [block for part in held for block in (part, swap(part, core))]


def collect(parts):
    steps = bits_of("fsdp")
    kind = parts[0].dtype
    core = steps[-1]
    held = []
    for i in range(0, len(parts), 2):
        arrived = swap(parts[i + 1], core)
        held.append((parts[i].astype(F32) + arrived.astype(F32)).astype(kind))
    for step in steps[:-1]:
        half = len(held) // 2
        held = [
            (held[i].astype(F32) + swap(held[half + i], step).astype(F32)).astype(kind)
            for i in range(half)
        ]
    return held[0]


def on_device(
    tokens,
    cotangent,
    project_in,
    project_out,
    router,
    first_gain,
    second_gain,
    bias_table,
    expert_up,
    expert_down,
    positions,
    buckets,
    routes,
    slots,
):
    highest = lax.Precision.HIGHEST
    count, width = tokens.shape
    experts = lax.axis_size("expert")
    capacity = 3 * count // experts
    rows_here = experts * capacity
    share = project_in.shape[0]
    mine = lax.axis_index("fsdp") * experts + lax.axis_index("expert")

    fbits, ebits = bits_of("fsdp"), bits_of("expert")
    order_a = ebits[:-1] + fbits[:-1] + ebits[-1:] + fbits[-1:]
    order_b = ebits + fbits

    half = project_in.shape[1] // 2
    small = jnp.concatenate(
        [
            router,
            first_gain[:, None],
            second_gain[:, None],
            jnp.zeros((share, LANES - experts - 2), BF),
        ],
        axis=1,
    )
    in_a = gather_blocks(project_in[:, :half], order_a)
    in_b = gather_blocks(project_in[:, half:], order_b)
    small_rel = gather_blocks(small, order_a)
    late_out, _ = lax.optimization_barrier((project_out, in_a))
    output_weight = gather_blocks(late_out, order_b)

    place = jnp.arange(width, dtype=jnp.int32)
    place_of = ((place // share) ^ mine) * share + place % share
    shuffle = (place[:, None] == place_of[None, :]).astype(BF)

    inputs = tokens.astype(F32)
    upstream = cotangent.astype(F32)
    inputs_rel = matmul(tokens, shuffle)

    target = routes * capacity + slots
    slot_index = jnp.arange(rows_here, dtype=jnp.int32)
    hot = (slot_index[None, None, :] == jnp.transpose(target)[:, :, None]).astype(BF)
    place_hot = hot[0] + hot[1]
    route_hot = (routes[:, :, None] == jnp.arange(experts, dtype=jnp.int32)).astype(F32)
    grad_out_rows = contract_rows(place_hot, cotangent).astype(BF)

    places = jnp.arange(count, dtype=jnp.int32)
    distance = places[:, None] - places[None, :]
    valid = (distance >= 0) & (distance <= positions[:, None])
    clipped = jnp.clip(distance, 0, count - 1)
    bucket_pair = jnp.sum(
        jnp.where(clipped[:, :, None] == places[None, None, :], buckets[None, None, :], 0), axis=-1
    )
    bucket_hot = (bucket_pair[:, :, None] == jnp.arange(BUCKETS, dtype=jnp.int32)).astype(F32)
    bias = jnp.einsum("qkb,bh->hqk", bucket_hot, bias_table, precision=highest)

    small_abs = lax.dot_general(
        small_rel, shuffle, (((0,), (1,)), ((), ())), preferred_element_type=F32
    )
    router_rows = small_abs[:experts].astype(BF)
    gain_second = small_abs[experts + 1]
    gain_rel = small_rel[:, experts].astype(F32)
    normed_rel = rms_scale(inputs_rel, gain_rel).astype(BF)
    joint = jnp.concatenate([matmul(normed_rel, in_a), matmul(normed_rel, in_b)], axis=1).astype(BF)
    query = joint[:, :width].reshape(count, HEADS, HEAD)
    keys_low = joint[:, width : 2 * width].reshape(count, HEADS, HEAD)
    values_low = joint[:, 2 * width :].reshape(count, HEADS, HEAD)
    raw = jnp.einsum("qhd,khd->hqk", query, keys_low, preferred_element_type=F32)
    scores = jnp.where(valid[None], raw * 0.125 + bias, -1e30)
    top = jnp.max(scores, axis=-1, keepdims=True)
    log_total = top + jnp.log(jnp.sum(jnp.exp(scores - top), axis=-1, keepdims=True))
    probs = jnp.exp(scores - log_total)
    probs_low = probs.astype(BF)
    attended = (
        jnp.einsum("hqk,khd->qhd", probs_low, values_low, preferred_element_type=F32)
        .astype(BF)
        .reshape(count, width)
    )
    attended_rel = matmul(attended, shuffle).astype(BF)
    first = inputs + matmul(attended_rel, output_weight)
    second_low = rms_scale(first, gain_second).astype(BF)

    rows_own = exchange(contract_rows(place_hot, second_low).astype(BF))
    rows_blocks = spread(rows_own)
    grad_blocks = spread(exchange(grad_out_rows))

    logits = contract_cols(second_low, router_rows)
    chosen = jnp.sum(logits[:, None, :] * route_hot, axis=-1)
    gates = jax.nn.softmax(chosen, axis=1)
    hot_f32 = hot.astype(F32)
    gate_slots = jnp.sum(hot_f32 * jnp.transpose(gates)[:, :, None], axis=(0, 1))
    gate_blocks = spread(exchange(gate_slots))

    weight_up, weight_down = expert_up[0], expert_down[0]
    active_blocks, inner_grads, row_grads, results, gate_dots = [], [], [], [], []
    for rows, grad in zip(rows_blocks, grad_blocks):
        inner = matmul(rows, weight_up)
        activated, pull = jax.vjp(jax.nn.gelu, inner)
        active_low = activated.astype(BF)
        inner_grad = pull(contract_cols(grad, weight_down))[0].astype(BF)
        result = matmul(active_low, weight_down)
        active_blocks.append(active_low)
        inner_grads.append(inner_grad)
        row_grads.append(contract_cols(inner_grad, weight_up).astype(BF))
        gate_dots.append(jnp.sum(result * grad.astype(F32), axis=-1))
        results.append(result.astype(BF))
    home_grad = exchange(collect(row_grads))
    gate_home = exchange(collect(gate_dots))
    returned = exchange(collect(results))

    gate_rows = jnp.concatenate(gate_blocks)[:, None]
    scaled_inner = (jnp.concatenate(inner_grads).astype(F32) * gate_rows).astype(BF)
    scaled_grad = (jnp.concatenate(grad_blocks).astype(F32) * gate_rows).astype(BF)
    grad_up = contract_rows(jnp.concatenate(rows_blocks), scaled_inner)
    grad_down = contract_rows(jnp.concatenate(active_blocks), scaled_grad)

    gate_grad = jnp.transpose(jnp.sum(hot_f32 * gate_home, axis=-1))
    chosen_grad = gates * (gate_grad - jnp.sum(gates * gate_grad, axis=1, keepdims=True))
    logit_grad = jnp.sum(route_hot * chosen_grad[:, :, None], axis=1).astype(BF)
    second_grad = (
        gates[:, 0:1] * matmul(hot[0], home_grad)
        + gates[:, 1:2] * matmul(hot[1], home_grad)
        + matmul(logit_grad, router_rows)
    )
    grad_router = contract_rows(second_low, logit_grad)
    branch_grad, gain_second_grad = jax.vjp(rms_scale, first, gain_second)[1](second_grad)
    first_grad = upstream + branch_grad
    first_low = first_grad.astype(BF)
    small_grad = jnp.concatenate(
        [
            grad_router,
            gain_second_grad[:, None],
            jnp.zeros((width, LANES - experts - 1), F32),
        ],
        axis=1,
    ).astype(BF)
    grad_out_local = jnp.concatenate(
        [
            contract_rows(attended_rel, first_low).astype(BF),
            contract_rows(shuffle, small_grad).astype(BF),
        ],
        axis=1,
    )
    attended_grad_rel = contract_cols(first_low, output_weight).astype(BF)
    attended_grad = contract_cols(attended_grad_rel, shuffle).astype(BF).reshape(count, HEADS, HEAD)
    prob_grad = jnp.einsum("qhd,khd->hqk", attended_grad, values_low, preferred_element_type=F32)
    score_grad = probs * (prob_grad - jnp.sum(probs * prob_grad, axis=-1, keepdims=True))
    table_grad = jnp.einsum("qkb,hqk->bh", bucket_hot, score_grad, precision=highest)
    pair_grad = (score_grad * 0.125).astype(BF)
    query_grad = jnp.einsum("hqk,khd->qhd", pair_grad, keys_low, preferred_element_type=F32)
    key_grad = jnp.einsum("hqk,qhd->khd", pair_grad, query, preferred_element_type=F32)
    value_grad = jnp.einsum("hqk,qhd->khd", probs_low, attended_grad, preferred_element_type=F32)
    joint_grad = jnp.concatenate(
        [
            query_grad.reshape(count, width),
            key_grad.reshape(count, width),
            value_grad.reshape(count, width),
        ],
        axis=1,
    ).astype(BF)
    back_a, back_b = order_a[::-1], order_b[::-1]
    sum_out = scatter_blocks(grad_out_local, back_b)
    sum_a = scatter_blocks(contract_rows(normed_rel, joint_grad[:, :half]).astype(BF), back_a)
    sum_b = scatter_blocks(contract_rows(normed_rel, joint_grad[:, half:]).astype(BF), back_b)
    grad_in = jnp.concatenate([sum_a, sum_b], axis=1)
    grad_first_gain = jnp.sum(grad_in * project_in.astype(F32), axis=1) / first_gain.astype(F32)

    normed_grad = contract_cols(joint_grad[:, :half], in_a) + contract_cols(joint_grad[:, half:], in_b)
    input_grad_rel = jax.vjp(lambda v: rms_scale(v, gain_rel), inputs_rel)[1](normed_grad)[0]
    high = input_grad_rel.astype(BF)
    rest = (input_grad_rel - high.astype(F32)).astype(BF)
    input_grad = contract_cols(high, shuffle) + contract_cols(rest, shuffle)
    token_grad = (first_grad + input_grad).astype(BF)

    routed = jnp.stack([matmul(hot[0], returned), matmul(hot[1], returned)])
    mixed = (first + jnp.sum(jnp.transpose(gates)[:, :, None] * routed, axis=0)).astype(BF)
    table_total = total_over_all(table_grad)
    return (
        mixed,
        token_grad,
        grad_in,
        sum_out[:, :width],
        sum_out[:, width : width + experts],
        grad_first_gain,
        sum_out[:, width + experts],
        table_total,
        grad_up[None],
        grad_down[None],
    )


def solution(mesh):
    rows = P(("fsdp", "expert"), None)
    line = P(("fsdp", "expert"))
    up, down = P("expert", None, "fsdp"), P("expert", "fsdp", None)
    return jax.shard_map(
        on_device,
        mesh=mesh,
        in_specs=(rows, rows, rows, rows, rows, line, line, P(), up, down, line, P(), rows, rows),
        out_specs=(rows, rows, rows, rows, rows, line, line, P(), up, down),
        check_vma=False,
    )
```

```python
import functools
import math

import jax
import jax.numpy as jnp
import numpy as np
from jax import lax
from jax.experimental import pallas as pl
from jax.experimental.pallas import tpu as pltpu
from jax.sharding import PartitionSpec as P

HEADS = 12
HEAD = 64
BUCKETS = 32
LANES = 128
BF = jnp.bfloat16
F32 = jnp.float32


def rms_scale(value, gain):
    return value * lax.rsqrt(jnp.mean(value * value, axis=-1, keepdims=True) + 1e-06) * gain


def contract_rows(left, right):
    return lax.dot_general(left, right, (((0,), (0,)), ((), ())), preferred_element_type=F32)


def contract_cols(left, right):
    return lax.dot_general(left, right, (((1,), (1,)), ((), ())), preferred_element_type=F32)


def matmul(left, right):
    return jnp.dot(left, right, preferred_element_type=F32)


AXES = ("fsdp", "expert")


def sizes():
    return lax.axis_size("fsdp"), lax.axis_size("expert")


def core_mask():
    return sizes()[1]


def xy_masks():
    columns, experts = sizes()
    return [2 * experts * x + y for y in range(2) for x in range(columns // 2)]


def chip_masks():
    columns, experts = sizes()
    return [2 * experts * x for x in range(columns // 2)]


def z_masks():
    return [2 * z for z in range(sizes()[1] // 2)]


def block_masks():
    return [c + xy + z for c in (0, core_mask()) for xy in xy_masks() for z in z_masks()]


def swap(value, mask):
    columns, experts = sizes()
    return lax.ppermute(value, AXES, [(i, i ^ mask) for i in range(columns * experts)])


def tied(value, other):
    return lax.optimization_barrier((value, other))[0]


def fan(value, masks):
    return [value] + [swap(value, mask) for mask in masks[1:]]


def fan_sum(parts, masks):
    arrived = [swap(part, mask) for part, mask in zip(parts[1:], masks[1:])]
    total = parts[0].astype(F32)
    for part in arrived:
        total = total + part.astype(F32)
    return total


def stack(parts):
    return jnp.concatenate(parts, axis=0)


def after(value, *others):
    return pl.pallas_call(
        lambda *refs: None,
        out_shape=jax.ShapeDtypeStruct(value.shape, value.dtype),
        in_specs=[pl.BlockSpec(memory_space=pl.ANY)] * (1 + len(others)),
        out_specs=pl.BlockSpec(memory_space=pl.ANY),
        input_output_aliases={0: 0},
    )(value, *others)


def gather_blocks(value, beside):
    value = stack(fan(value, z_masks()))
    value = stack(fan(after(value, beside), xy_masks()))
    return value, swap(value, core_mask())


def add_low(own, arrived):
    return (own.astype(F32) + arrived.astype(F32)).astype(BF)


def scatter_blocks(value):
    xy, z = xy_masks(), z_masks()
    value = value.reshape(len(xy), -1, value.shape[1])
    arrived = [swap(value[i], xy[i]) for i in range(1, len(xy))]
    value = sum((part.astype(F32) for part in arrived), value[0].astype(F32)).astype(BF)
    value = value.reshape(len(z), -1, value.shape[1])
    return [value[0]] + [swap(value[i], z[i]) for i in range(1, len(z))], arrived[0]


def exchange(value):
    experts = lax.axis_size("expert")
    blocks = value.reshape(experts, value.shape[0] // experts, value.shape[1])
    moved = lax.all_to_all(blocks, "expert", split_axis=0, concat_axis=0, tiled=True)
    return moved.reshape(value.shape)


def lanes_of(value, place):
    high = value.astype(BF)
    rest = (value - high.astype(F32)).astype(BF)
    lane = lax.broadcasted_iota(jnp.int32, (value.shape[0], LANES), 1)
    nothing = jnp.zeros((), BF)
    return jnp.where(lane == place, high, jnp.where(lane == place + 1, rest, nothing))


def nt(left, right):
    return contract_cols(left, right)


def tn(left, right):
    return contract_rows(left, right)


class Incoming:
    def __init__(self, ref, copy):
        self.ref, self.copy = ref, copy
        self.shape, self.dtype = ref.shape, ref.dtype
        copy.start()

    def wait(self):
        if self.copy is not None:
            self.copy.wait()
            self.copy = None

    def __getitem__(self, index):
        self.wait()
        return self.ref[index]


def kernel_call(body, outs, flops, *operands, fetch=(), scratch=16):
    moved = sum(math.prod(v.shape) * v.dtype.itemsize for v in operands)
    moved += sum(math.prod(shape) * jnp.dtype(kind).itemsize for shape, kind in outs)
    taken = len(operands) + len(outs)

    def kernel(*refs):
        refs, buffers = list(refs[:taken]), refs[taken:]
        for i, number in enumerate(fetch):
            copy = pltpu.make_async_copy(refs[number], buffers[i], buffers[-1].at[i])
            refs[number] = Incoming(buffers[i], copy)
        body(*refs)
        for number in fetch:
            refs[number].wait()

    whole, left = pl.BlockSpec(memory_space=pltpu.VMEM), pl.BlockSpec(memory_space=pl.ANY)
    buffers = [pltpu.VMEM(operands[i].shape, operands[i].dtype) for i in fetch]
    if fetch:
        buffers.append(pltpu.SemaphoreType.DMA((len(fetch),)))
    return pl.pallas_call(
        kernel,
        out_shape=[jax.ShapeDtypeStruct(shape, kind) for shape, kind in outs],
        in_specs=[left if i in fetch else whole for i in range(len(operands))],
        out_specs=[whole] * len(outs),
        scratch_shapes=buffers,
        compiler_params=pltpu.CompilerParams(vmem_limit_bytes=scratch * 1024 * 1024),
        cost_estimate=pl.CostEstimate(flops=flops, bytes_accessed=moved, transcendentals=0),
    )(*operands)


def pick_heads(first_head, second_head):
    lane = lax.broadcasted_iota(jnp.int32, first_head.shape, 1)
    return jnp.where(lane < HEAD, first_head, second_head)


def one_head(pair, side):
    lane = lax.broadcasted_iota(jnp.int32, pair.shape, 1)
    return jnp.where((lane < HEAD) == (side == 0), pair, jnp.zeros((), pair.dtype))


def pair_of(value, number):
    return value[:, number * LANES : (number + 1) * LANES]


def inverse_rms(value):
    return lax.rsqrt(jnp.mean(value * value, axis=-1, keepdims=True) + 1e-06)


def shuffle_of(place_of):
    width = place_of.shape[1]
    return (lax.broadcasted_iota(jnp.int32, (width, width), 0) == place_of[...]).astype(BF)


def small_of(near, far, shuffle):
    lanes = near.shape[1] - 4 * shuffle.shape[0]
    rows = jnp.concatenate([near[:, :lanes], far[:, :lanes]], axis=0)
    return jnp.transpose(matmul(shuffle, rows)).astype(BF)


def pack_kernel(router_rows, first_gain, second_gain, project_in, project_out, packed_ref):
    share, columns = project_in.shape
    experts = router_rows.shape[0]
    at = packed_ref.shape[1] - columns - project_out.shape[1]
    eye = lax.broadcasted_iota(jnp.int32, (share, share), 0)
    eye = (eye == lax.broadcasted_iota(jnp.int32, (share, share), 1)).astype(BF)
    rows = jnp.concatenate(
        [router_rows[...], first_gain[...], second_gain[...], jnp.zeros((at - experts - 2, share), BF)],
        axis=0,
    )
    packed_ref[:, :at] = nt(eye, rows).astype(BF)
    packed_ref[:, at : at + columns] = project_in[...]
    packed_ref[:, at + columns :] = project_out[...]


def forward_kernel(
    experts,
    tokens,
    place_of,
    near,
    far,
    bias_rows,
    positions,
    routes,
    target_rows,
    low_ref,
    high_ref,
    outgoing_ref,
):
    count, width = tokens.shape
    at_probs = width + LANES
    shuffle = shuffle_of(place_of)
    small = small_of(near, far, shuffle)
    half = width // 2
    inputs = tokens[...].astype(F32)
    gain_first = small[experts : experts + 1].astype(F32)
    gain_second = small[experts + 1 : experts + 2].astype(F32)
    normed = (inputs * inverse_rms(inputs) * gain_first).astype(BF)
    normed = matmul(normed, shuffle).astype(BF)
    low_ref[:, 3 * width : 4 * width] = normed
    at = near.shape[1] - 4 * width
    joint = matmul(normed[:, :half], near[:, at : at + 3 * width])
    joint = joint + matmul(normed[:, half:], far[:, at : at + 3 * width])
    low_ref[:, : 3 * width] = joint.astype(BF)
    row = lax.broadcasted_iota(jnp.int32, (count, count), 0)
    distance = row - lax.broadcasted_iota(jnp.int32, (count, count), 1)
    valid = (distance >= 0) & (distance <= positions[...])
    pairs = width // LANES
    attended = []
    for number in range(pairs):
        query, keys, values = (
            low_ref[:, i * width + number * LANES : i * width + (number + 1) * LANES] for i in range(3)
        )
        outs = []
        for side in range(2):
            head = 2 * number + side
            bias = jnp.broadcast_to(bias_rows[head : head + 1], (count, count))
            bias = pltpu.roll(bias, 0, 1, stride=1, stride_axis=0)
            scores = jnp.where(valid, nt(one_head(query, side), keys) * 0.125 + bias, -1e30)
            expo = jnp.exp(scores - jnp.max(scores, axis=-1, keepdims=True))
            probs = expo / jnp.sum(expo, axis=-1, keepdims=True)
            high_ref[:, at_probs + head * count : at_probs + (head + 1) * count] = probs
            outs.append(matmul(probs.astype(BF), values))
        attended.append(pick_heads(*outs).astype(BF))
    attended = matmul(jnp.concatenate(attended, axis=1), shuffle).astype(BF)
    low_ref[:, 4 * width : 5 * width] = attended
    first = inputs + matmul(attended[:, :half], near[:, at + 3 * width :])
    first = first + matmul(attended[:, half:], far[:, at + 3 * width :])
    high_ref[:, :width] = first
    second = (first * inverse_rms(first) * gain_second).astype(BF)
    low_ref[:, 5 * width :] = second
    logits = nt(second, small[:LANES])
    lane = lax.broadcasted_iota(jnp.int32, logits.shape, 1)
    chosen = [
        jnp.sum(jnp.where(lane == routes[:, c : c + 1], logits, 0.0), axis=-1, keepdims=True)
        for c in range(2)
    ]
    top = jnp.maximum(chosen[0], chosen[1])
    expo = [jnp.exp(value - top) for value in chosen]
    gates = [value / (expo[0] + expo[1]) for value in expo]
    high_ref[:, width:at_probs] = jnp.where(lane == 0, gates[0], jnp.where(lane == 1, gates[1], 0.0))
    slot = lax.broadcasted_iota(jnp.int32, (outgoing_ref.shape[0], count), 0)
    rows = jnp.zeros(outgoing_ref.shape, F32)
    for c in range(2):
        hot = (slot == target_rows[c : c + 1]).astype(BF)
        rows = rows + matmul(hot, jnp.concatenate([second, lanes_of(gates[c], 0)], axis=1))
    outgoing_ref[...] = rows.astype(BF)


def expert_forward(rows, up):
    inner = nt(rows, up)
    square = inner * inner
    bend = jnp.tanh(0.7978845608028654 * inner * (1.0 + 0.044715 * square))
    slope = 0.5 * (1.0 + bend) + 0.5 * inner * (1.0 - bend * bend) * (
        0.7978845608028654 * (1.0 + 0.134145 * square)
    )
    return (0.5 * inner * (1.0 + bend)).astype(BF), slope


def gate_of(packed, width):
    return packed[:, width : width + 1].astype(F32) + packed[:, width + 1 : width + 2].astype(F32)


def expert_kernel(chips, column, *refs):
    rows, grads, weights, refs = refs[:2], refs[2:4], refs[4 : 4 + chips], refs[4 + chips :]
    row_refs, result_ref, kept_ref = refs[:2], refs[2], refs[3]
    count, width = grads[0].shape
    hidden = weights[0].shape[0] // 2
    for core in range(2):
        packed, grad = rows[core], grads[core][...]
        gate = gate_of(packed, width)
        block = slice(core * count, (core + 1) * count)
        result, row_grad = jnp.zeros((count, width), F32), jnp.zeros((count, width), F32)
        for i in range(chips):
            up, down = weights[i][:hidden], weights[i][hidden:]
            active, slope = expert_forward(packed[:, :width], up)
            inner_grad = nt(grad, down) * slope
            if i == 0:
                kept_ref[block, :hidden] = active
                kept_ref[block, hidden : 2 * hidden] = (inner_grad * gate).astype(BF)
            result = result + matmul(active, down)
            row_grad = row_grad + matmul(inner_grad.astype(BF), up)
        grad = grad.astype(F32)
        kept_ref[block, 2 * hidden :] = (grad * gate).astype(BF)
        result_ref[block] = result.astype(BF)
        dots = jnp.sum(result * grad, axis=-1, keepdims=True)
        row_refs[core][...] = jnp.concatenate(
            [row_grad.astype(BF), lanes_of(dots, 2 * column[0, 0])], axis=1
        )


def weight_grad_kernel(others, weights, kept, far, near, *refs):
    packed_far, grads_far, (up_ref, down_ref) = refs[:others], refs[others : 2 * others], refs[2 * others :]
    width = up_ref.shape[0]
    hidden = up_ref.shape[1]
    count = near.shape[0]
    up, down = weights[:hidden], weights[hidden:]
    for i, rows in enumerate((far, near)):
        block = slice(i * count, (i + 1) * count)
        scaled = kept[block, 2 * hidden :]
        parts = (
            tn(rows[:, :width], kept[block, hidden : 2 * hidden]),
            tn(kept[block, :hidden], scaled),
        )
        if i == 0:
            up_ref[...], down_ref[...] = parts
        else:
            up_ref[...] += parts[0]
            down_ref[...] += parts[1]
    for packed, grad_ref in zip(packed_far, grads_far):
        gate = gate_of(packed, width)
        grad = grad_ref[...]
        active, slope = expert_forward(packed[:, :width], up)
        inner_grad = (nt(grad, down) * slope * gate).astype(BF)
        up_ref[...] += tn(packed[:, :width], inner_grad)
        down_ref[...] += tn(active, (grad.astype(F32) * gate).astype(BF))


def table_lanes(share):
    return BUCKETS * HEADS // share


def home_kernel(
    experts,
    share,
    home,
    routes,
    target,
    cotangent,
    place_of,
    low,
    high,
    near,
    far,
    flip_hot,
    keep_ref,
    send_ref,
    first_grad_ref,
    joint_grad_ref,
    distance_ref,
):
    count, width = cotangent.shape
    half = width // 2
    shuffle = shuffle_of(place_of)
    small_rows = small_of(near, far, shuffle)
    at_probs = width + LANES
    slot = lax.broadcasted_iota(jnp.int32, (count, home.shape[0]), 1)
    lane = lax.broadcasted_iota(jnp.int32, (count, LANES), 1)
    gates = [high[:, width + c : width + c + 1] for c in range(2)]
    routed = [matmul((slot == target[:, c : c + 1]).astype(BF), home[...]) for c in range(2)]
    dots = [jnp.sum(value[:, width:], axis=-1, keepdims=True) for value in routed]
    mean = gates[0] * dots[0] + gates[1] * dots[1]
    logit_grad = jnp.zeros((count, LANES), F32)
    for c in range(2):
        logit_grad = jnp.where(lane == routes[:, c : c + 1], gates[c] * (dots[c] - mean), logit_grad)
    logit_grad = logit_grad.astype(BF)
    second_grad = gates[0] * routed[0][:, :width] + gates[1] * routed[1][:, :width]
    second_grad = second_grad + matmul(logit_grad, small_rows[:LANES])
    gain = small_rows[experts + 1 : experts + 2].astype(F32)
    first = high[:, :width]
    inverse = inverse_rms(first)
    unit = first * inverse
    scaled = second_grad * gain
    first_grad = cotangent[...].astype(F32) + inverse * (
        scaled - unit * jnp.mean(unit * scaled, axis=-1, keepdims=True)
    )
    first_grad_ref[...] = first_grad
    first_low = first_grad.astype(BF)
    attended_grad = jnp.concatenate(
        [nt(first_low, part[:, part.shape[1] - width :]) for part in (near, far)], axis=1
    ).astype(BF)
    attended_grad = nt(attended_grad, shuffle).astype(BF)
    value_grad = []
    for number in range(width // LANES):
        outs = [
            tn(
                high[:, at_probs + head * count : at_probs + (head + 1) * count].astype(BF),
                pair_of(attended_grad, number),
            )
            for head in (2 * number, 2 * number + 1)
        ]
        value_grad.append(pick_heads(*outs).astype(BF))
    value_grad = jnp.concatenate(value_grad, axis=1)
    joint_grad_ref[:, 2 * width :] = value_grad
    gain_part = second_grad * unit
    gain_high = gain_part.astype(BF)
    gain_rest = (gain_part - gain_high.astype(F32)).astype(BF)
    ones = (lane == experts).astype(BF)
    left = jnp.concatenate([low[:, 5 * width :], gain_high, gain_rest], axis=0)
    left = matmul(left, shuffle).astype(BF)
    right = jnp.concatenate([logit_grad, ones, ones], axis=0)
    small = tn(left, right)
    row = lax.broadcasted_iota(jnp.int32, (count, count), 0)
    for number in range(width // LANES):
        span = slice(number * LANES, (number + 1) * LANES)
        query, keys, values = (
            low[:, i * width + number * LANES : i * width + (number + 1) * LANES] for i in range(3)
        )
        own_grad = attended_grad[:, span]
        query_grads, key_grads = [], []
        for side in range(2):
            head = 2 * number + side
            chance = high[:, at_probs + head * count : at_probs + (head + 1) * count]
            prob_grad = nt(one_head(own_grad, side), values)
            score_grad = chance * (prob_grad - jnp.sum(chance * prob_grad, axis=-1, keepdims=True))
            lined = score_grad
            step = 1
            while step < count:
                lined = jnp.where((row // step) % 2 == 1, pltpu.roll(lined, count - step, 1), lined)
                step *= 2
            distance_ref[head : head + 1] = jnp.sum(lined, axis=0, keepdims=True)
            pair_grad = (score_grad * 0.125).astype(BF)
            query_grads.append(matmul(pair_grad, keys))
            key_grads.append(tn(pair_grad, query))
        joint_grad_ref[:, span] = pick_heads(*query_grads).astype(BF)
        joint_grad_ref[:, width + number * LANES : width + (number + 1) * LANES] = pick_heads(
            *key_grads
        ).astype(BF)
    table = jnp.dot(
        distance_ref[...], flip_hot[...], precision=lax.Precision.HIGHEST, preferred_element_type=F32
    ).astype(BF)
    lanes = table_lanes(share)
    spread = keep_ref.shape[1] - 4 * width
    value_row = lax.broadcasted_iota(jnp.int32, (width, HEADS), 0) % share * lanes
    value_head = lax.broadcasted_iota(jnp.int32, (width, HEADS), 1)
    bucket = lax.broadcasted_iota(jnp.int32, (BUCKETS, spread), 0)
    lane = lax.broadcasted_iota(jnp.int32, (BUCKETS, spread), 1) - (experts + 1)
    small = jnp.pad(small, ((0, 0), (0, spread - LANES)))
    for start in range(0, max(lanes, BUCKETS), min(lanes, BUCKETS)):
        if lanes <= BUCKETS:
            picked = (value_row == value_head * BUCKETS + start).astype(BF)
            put = ((lane >= 0) & (lane < lanes) & (bucket == lane + start)).astype(BF)
        else:
            picked = (value_row + start == value_head * BUCKETS).astype(BF)
            put = (lane - start == bucket).astype(BF)
        small = small + matmul(picked, matmul(table, put).astype(BF))
    joint_grads = joint_grad_ref[...]
    for ref, at in ((keep_ref, 0), (send_ref, half)):
        attended, normed = (low[:, i * width + at : i * width + at + half] for i in (4, 3))
        ref[:, : 3 * width] = tn(normed, joint_grads).astype(BF)
        ref[:, 3 * width : 4 * width] = tn(attended, first_low).astype(BF)
        ref[:, 4 * width :] = small[at : at + half].astype(BF)


def finish_kernel(project_in, gain, *refs):
    parts, (grad_in_ref, sum_out_ref, small_ref, gain_ref) = refs[:-4], refs[-4:]
    sums = sum(part[...].astype(F32) for part in parts)
    width = sum_out_ref.shape[1]
    grad_in = sums[:, : 3 * width]
    grad_in_ref[...] = grad_in
    sum_out_ref[...] = sums[:, 3 * width : 4 * width]
    small_ref[...] = sums[:, 4 * width :]
    grads = grad_in * project_in[...].astype(F32)
    gain_ref[...] = jnp.sum(grads, axis=-1, keepdims=True) / gain[...].astype(F32)


def on_device(
    tokens,
    cotangent,
    project_in,
    project_out,
    router,
    first_gain,
    second_gain,
    bias_table,
    expert_up,
    expert_down,
    positions,
    buckets,
    routes,
    slots,
):
    highest = lax.Precision.HIGHEST
    count, width = tokens.shape
    experts = lax.axis_size("expert")
    capacity = 3 * count // experts
    rows_here = experts * capacity
    share = project_in.shape[0]
    column = lax.axis_index("fsdp")
    mine = column * experts + lax.axis_index("expert")
    small_lanes = -(-(experts + 2) // LANES) * LANES
    (packed,) = kernel_call(
        pack_kernel,
        [((share, small_lanes + 4 * width), BF)],
        0,
        router.T,
        first_gain[None],
        second_gain[None],
        project_in,
        project_out,
        fetch=range(5),
        scratch=56,
    )
    weights = stack([expert_up[0].T, expert_down[0]])
    halves = gather_blocks(packed, weights)
    weights = fan(after(weights, halves[0]), chip_masks())
    in_halves = [half[:, small_lanes : small_lanes + 3 * width] for half in halves]

    def times_back(value, parts):
        return jnp.concatenate([contract_cols(value, part) for part in parts], axis=1)

    feature = jnp.arange(width, dtype=jnp.int32)
    masks = jnp.asarray(np.repeat(np.array(block_masks(), np.int32), share))
    place_of = (masks ^ mine) * share + feature % share
    shuffle = (feature[:, None] == place_of[None, :]).astype(BF)

    inputs = tokens.astype(F32)
    inputs_rel = matmul(tokens, shuffle)

    target = routes * capacity + slots
    slot_index = jnp.arange(rows_here, dtype=jnp.int32)
    hot = (slot_index[None, None, :] == jnp.transpose(target)[:, :, None]).astype(BF)
    place_hot = hot[0] + hot[1]
    grad_rows = contract_rows(place_hot, cotangent).astype(BF)
    grad_own = exchange(grad_rows)
    grad_parts = (grad_own, swap(grad_own, core_mask()))

    places = jnp.arange(count, dtype=jnp.int32)
    bucket_hot = (buckets[:, None] == jnp.arange(BUCKETS, dtype=jnp.int32)).astype(F32)
    flip = ((places[:, None] + places[None, :]) % count == 0).astype(F32)
    flip_hot = jnp.dot(flip, bucket_hot, precision=highest)
    bias_rows = lax.dot_general(
        bias_table, flip_hot, (((0,), (1,)), ((), ())), precision=highest
    )
    low, high, outgoing = kernel_call(
        functools.partial(forward_kernel, experts),
        [
            ((count, 6 * width), BF),
            ((count, width + LANES + HEADS * count), F32),
            ((rows_here, width + LANES), BF),
        ],
        2 * count * width * 6 * width,
        tokens,
        place_of[None],
        *halves,
        bias_rows,
        positions[:, None],
        routes,
        jnp.transpose(target),
    )
    row_own = exchange(after(outgoing, grad_own))
    row_parts = (row_own, swap(row_own, core_mask()))

    chips = len(chip_masks())
    piece = expert_up.shape[2]
    wide = (rows_here, width + LANES)
    row_far, row_near, result, kept = kernel_call(
        functools.partial(expert_kernel, chips),
        [(wide, BF), (wide, BF), ((2 * rows_here, width), BF), ((2 * rows_here, 2 * piece + width), BF)],
        16 * rows_here * width * chips * piece,
        column.astype(jnp.int32).reshape(1, 1),
        row_parts[1],
        row_parts[0],
        grad_parts[1],
        grad_parts[0],
        *weights,
        fetch=range(5, 5 + len(weights)),
        scratch=56,
    )
    home = exchange(add_low(row_near, swap(row_far, core_mask())))
    result_own = add_low(result[rows_here:], swap(result[:rows_here], core_mask()))

    far = []
    for own in (row_own, grad_own):
        parts = [swap(after(own, *weights[1:]), mask) for mask in chip_masks()[1:]]
        far += [both for part in parts for both in (part, swap(part, core_mask()))]
    home = after(home, result_own, *far)

    half = width // 2
    table_at = experts + 1
    spread_lanes = -(-(table_at + table_lanes(share)) // LANES) * LANES
    keep, send, first_grad, joint_grad, _ = kernel_call(
        functools.partial(home_kernel, experts, share),
        [
            ((half, 4 * width + spread_lanes), BF),
            ((half, 4 * width + spread_lanes), BF),
            ((count, width), F32),
            ((count, 3 * width), BF),
            ((HEADS, count), F32),
        ],
        2 * count * width * 10 * width,
        home,
        routes,
        target,
        cotangent,
        place_of[None],
        low,
        high,
        *halves,
        flip_hot,
        fetch=(7, 8, 6, 3, 5),
        scratch=56,
    )
    dense_half = add_low(keep, swap(send, core_mask()))
    blocks, phase = scatter_blocks(dense_half)
    grad_up, grad_down = kernel_call(
        functools.partial(weight_grad_kernel, len(far) // 2),
        [((width, piece), F32), ((piece, width), F32)],
        16 * rows_here * width * chips * piece,
        weights[0],
        after(kept, dense_half),
        row_parts[1],
        row_parts[0],
        *far,
        fetch=range(4 + len(far)),
        scratch=56,
    )
    normed_grad = times_back(after(joint_grad, phase), in_halves)
    gain_rel = stack([part[:, experts] for part in halves]).astype(F32)
    input_grad_rel = jax.vjp(lambda v: rms_scale(v, gain_rel), inputs_rel)[1](normed_grad)[0]
    large = input_grad_rel.astype(BF)
    rest = (input_grad_rel - large.astype(F32)).astype(BF)
    input_grad = contract_cols(large, shuffle) + contract_cols(rest, shuffle)
    token_grad = (first_grad + input_grad).astype(BF)

    returned = exchange(after(result_own, token_grad))
    routed = [matmul(hot[c], returned) for c in range(2)]
    first, gates = high[:, :width], high[:, width : width + 2]
    mixed = (first + gates[:, 0:1] * routed[0] + gates[:, 1:2] * routed[1]).astype(BF)
    grad_in, sum_out, sum_small, grad_first_gain = kernel_call(
        finish_kernel,
        [
            ((share, 3 * width), F32),
            ((share, width), F32),
            ((share, spread_lanes), F32),
            ((share, 1), F32),
        ],
        share * width * 8,
        project_in,
        first_gain[:, None],
        after(blocks[0], mixed),
        *blocks[1:],
    )
    table_total = sum_small[:, table_at : table_at + table_lanes(share)]
    table_total = table_total.reshape(HEADS, BUCKETS).T
    return (
        mixed,
        token_grad,
        grad_in,
        sum_out,
        sum_small[:, :experts],
        grad_first_gain[:, 0],
        sum_small[:, experts],
        table_total,
        grad_up[None],
        grad_down[None],
    )


def solution(mesh):
    rows = P(("fsdp", "expert"), None)
    line = P(("fsdp", "expert"))
    up, down = P("expert", None, "fsdp"), P("expert", "fsdp", None)
    return jax.shard_map(
        on_device,
        mesh=mesh,
        in_specs=(rows, rows, rows, rows, rows, line, line, P(), up, down, line, P(), rows, rows),
        out_specs=(rows, rows, rows, rows, rows, line, line, P(), up, down),
        check_vma=False,
    )
```

```python
import functools
import math

import jax
import jax.numpy as jnp
import numpy as np
from jax import lax
from jax.experimental import pallas as pl
from jax.experimental.pallas import tpu as pltpu
from jax.sharding import PartitionSpec as P

HEADS = 12
HEAD = 64
BUCKETS = 32
LANES = 128
BF = jnp.bfloat16
F32 = jnp.float32


def rms_scale(value, gain):
    return value * lax.rsqrt(jnp.mean(value * value, axis=-1, keepdims=True) + 1e-06) * gain


def contract_rows(left, right):
    return lax.dot_general(left, right, (((0,), (0,)), ((), ())), preferred_element_type=F32)


def contract_cols(left, right):
    return lax.dot_general(left, right, (((1,), (1,)), ((), ())), preferred_element_type=F32)


def matmul(left, right):
    return jnp.dot(left, right, preferred_element_type=F32)


AXES = ("fsdp", "expert")


def sizes():
    return lax.axis_size("fsdp"), lax.axis_size("expert")


def core_mask():
    return sizes()[1]


def xy_masks():
    columns, experts = sizes()
    return [2 * experts * x + y for y in range(2) for x in range(columns // 2)]


def chip_masks():
    columns, experts = sizes()
    return [2 * experts * x for x in range(columns // 2)]


def z_masks():
    return [2 * z for z in range(sizes()[1] // 2)]


def block_masks():
    return [c + xy + z for c in (0, core_mask()) for xy in xy_masks() for z in z_masks()]


def swap(value, mask):
    columns, experts = sizes()
    return lax.ppermute(value, AXES, [(i, i ^ mask) for i in range(columns * experts)])


def tied(value, other):
    return lax.optimization_barrier((value, other))[0]


def fan(value, masks):
    return [value] + [swap(value, mask) for mask in masks[1:]]


def stack(parts):
    return jnp.concatenate(parts, axis=0)


def after(value, *others):
    return pl.pallas_call(
        lambda *refs: None,
        out_shape=jax.ShapeDtypeStruct(value.shape, value.dtype),
        in_specs=[pl.BlockSpec(memory_space=pl.ANY)] * (1 + len(others)),
        out_specs=pl.BlockSpec(memory_space=pl.ANY),
        input_output_aliases={0: 0},
    )(value, *others)


def gather_blocks(value, early, late):
    value = stack(fan(value, z_masks()))
    value = after(stack(fan(after(value, *early), xy_masks())), *late)
    return value, swap(value, core_mask())


def add_low(own, arrived):
    return (own.astype(F32) + arrived.astype(F32)).astype(BF)


def sum_kernel(inputs, *refs):
    total = sum((ref[...].astype(F32) for ref in refs[1:inputs]), refs[0][...].astype(F32))
    rows = total.shape[0] // (len(refs) - inputs)
    for i, ref in enumerate(refs[inputs:]):
        ref[...] = total[i * rows : (i + 1) * rows].astype(BF)


def sum_apart(parts, pieces):
    rows, width = parts[0].shape
    outs = [((rows // pieces, width), BF)] * pieces
    return kernel_call(functools.partial(sum_kernel, len(parts)), outs, rows * width, *parts)


def scatter_blocks(value, other, meanwhile):
    xy, z = xy_masks(), z_masks()
    parts = sum_apart([value, swap(other, core_mask())], len(xy))
    arrived = fan_sends(parts, xy)
    done = meanwhile(parts[0])
    sums = sum_apart([after(parts[0], *done), *arrived], len(z))
    return [sums[0], *fan_sends(sums, z)], done


def fan_sends(parts, masks):
    return [swap(part, mask) for part, mask in zip(parts[1:], masks[1:])]


def exchange(value):
    experts = lax.axis_size("expert")
    blocks = value.reshape(experts, value.shape[0] // experts, value.shape[1])
    moved = lax.all_to_all(blocks, "expert", split_axis=0, concat_axis=0, tiled=True)
    return moved.reshape(value.shape)


def lanes_of(value, place):
    high = value.astype(BF)
    rest = (value - high.astype(F32)).astype(BF)
    lane = lax.broadcasted_iota(jnp.int32, (value.shape[0], LANES), 1)
    nothing = jnp.zeros((), BF)
    return jnp.where(lane == place, high, jnp.where(lane == place + 1, rest, nothing))


def nt(left, right):
    return contract_cols(left, right)


def tn(left, right):
    return contract_rows(left, right)


class Incoming:
    def __init__(self, ref, copy):
        self.ref, self.copy = ref, copy
        self.shape, self.dtype = ref.shape, ref.dtype
        copy.start()

    def wait(self):
        if self.copy is not None:
            self.copy.wait()
            self.copy = None

    def __getitem__(self, index):
        self.wait()
        return self.ref[index]


def kernel_call(body, outs, flops, *operands, fetch=(), push=(), scratch=16):
    moved = sum(math.prod(v.shape) * v.dtype.itemsize for v in operands)
    moved += sum(math.prod(shape) * jnp.dtype(kind).itemsize for shape, kind in outs)
    taken = len(operands)
    fetch = [
        item if isinstance(item, tuple) else (item, ..., operands[item].shape) for item in fetch
    ]
    push = list(push)

    def kernel(*refs):
        buffers, refs = refs[taken + len(outs) :], list(refs[: taken + len(outs)])
        arriving, leaving, sent = [], {}, []
        for i, (number, index, _) in enumerate(fetch):
            source = refs[number] if index is ... else refs[number].at[index]
            copy = pltpu.make_async_copy(source, buffers[i], buffers[-1].at[i])
            refs[number] = Incoming(buffers[i], copy)
            arriving.append(refs[number])
        for i, number in enumerate(push, len(fetch)):
            leaving[number] = pltpu.make_async_copy(
                buffers[i], refs[taken + number], buffers[-1].at[i]
            )
            refs[taken + number] = buffers[i]

        def send(number):
            leaving[number].start()
            sent.append(number)

        body(*refs, *([send] if push else []))
        for number in push:
            if number not in sent:
                send(number)
        for value in arriving:
            value.wait()
        for number in push:
            leaving[number].wait()

    whole, left = pl.BlockSpec(memory_space=pltpu.VMEM), pl.BlockSpec(memory_space=pl.ANY)
    fetched = [number for number, _, _ in fetch]
    buffers = [pltpu.VMEM(shape, operands[number].dtype) for number, _, shape in fetch]
    buffers += [pltpu.VMEM(*outs[number]) for number in push]
    if buffers:
        buffers.append(pltpu.SemaphoreType.DMA((len(buffers),)))
    return pl.pallas_call(
        kernel,
        out_shape=[jax.ShapeDtypeStruct(shape, kind) for shape, kind in outs],
        in_specs=[left if i in fetched else whole for i in range(taken)],
        out_specs=[left if i in push else whole for i in range(len(outs))],
        scratch_shapes=buffers,
        compiler_params=pltpu.CompilerParams(vmem_limit_bytes=scratch * 1024 * 1024),
        cost_estimate=pl.CostEstimate(flops=flops, bytes_accessed=moved, transcendentals=0),
    )(*operands)


def pick_heads(first_head, second_head):
    lane = lax.broadcasted_iota(jnp.int32, first_head.shape, 1)
    return jnp.where(lane < HEAD, first_head, second_head)


def one_head(pair, side):
    lane = lax.broadcasted_iota(jnp.int32, pair.shape, 1)
    return jnp.where((lane < HEAD) == (side == 0), pair, jnp.zeros((), pair.dtype))


def pair_of(value, number):
    return value[:, number * LANES : (number + 1) * LANES]


def inverse_rms(value):
    return lax.rsqrt(jnp.mean(value * value, axis=-1, keepdims=True) + 1e-06)


def small_lanes(experts):
    return -(-(experts + 2) // LANES) * LANES


def shuffle_of(place_of):
    width = place_of.shape[1]
    return (lax.broadcasted_iota(jnp.int32, (width, width), 0) == place_of[...]).astype(BF)


def small_of(lanes, near, far, shuffle):
    end = near.shape[1] - shuffle.shape[0]
    start = end - lanes
    rows = jnp.concatenate([near[:, start:end], far[:, start:end]], axis=0)
    return jnp.transpose(matmul(shuffle, rows)).astype(BF)


def pack_kernel(
    router_rows, first_gain, second_gain, project_in, project_out, down, packed_ref, down_ref
):
    share, columns = project_in.shape
    experts = router_rows.shape[0]
    lanes = packed_ref.shape[1] - columns - project_out.shape[1]
    eye = lax.broadcasted_iota(jnp.int32, (share, share), 0)
    eye = (eye == lax.broadcasted_iota(jnp.int32, (share, share), 1)).astype(BF)
    rows = jnp.concatenate(
        [router_rows[...], first_gain[...], second_gain[...], jnp.zeros((lanes - experts - 2, share), BF)],
        axis=0,
    )
    packed_ref[:, :columns] = project_in[...]
    packed_ref[:, columns : columns + lanes] = nt(eye, rows).astype(BF)
    packed_ref[:, columns + lanes :] = project_out[...]
    down_ref[...] = down[...]


def forward_kernel(
    experts,
    tokens,
    place_of,
    near,
    far,
    bias_rows,
    positions,
    routes,
    target_rows,
    low_ref,
    high_ref,
    outgoing_ref,
    send,
):
    count, width = tokens.shape
    at_probs = width + LANES
    shuffle = shuffle_of(place_of)
    small = small_of(small_lanes(experts), near, far, shuffle)
    half = width // 2
    inputs = tokens[...].astype(F32)
    gain_first = small[experts : experts + 1].astype(F32)
    gain_second = small[experts + 1 : experts + 2].astype(F32)
    normed = (inputs * inverse_rms(inputs) * gain_first).astype(BF)
    normed = matmul(normed, shuffle).astype(BF)
    low_ref[:, 3 * width : 4 * width] = normed
    joint = matmul(normed[:, :half], near[:, : 3 * width])
    joint = joint + matmul(normed[:, half:], far[:, : 3 * width])
    low_ref[:, : 3 * width] = joint.astype(BF)
    row = lax.broadcasted_iota(jnp.int32, (count, count), 0)
    distance = row - lax.broadcasted_iota(jnp.int32, (count, count), 1)
    valid = (distance >= 0) & (distance <= positions[...])
    pairs = width // LANES
    attended = []
    for number in range(pairs):
        query, keys, values = (
            low_ref[:, i * width + number * LANES : i * width + (number + 1) * LANES] for i in range(3)
        )
        outs = []
        for side in range(2):
            head = 2 * number + side
            bias = jnp.broadcast_to(bias_rows[head : head + 1], (count, count))
            bias = pltpu.roll(bias, 0, 1, stride=1, stride_axis=0)
            scores = jnp.where(valid, nt(one_head(query, side), keys) * 0.125 + bias, -1e30)
            expo = jnp.exp(scores - jnp.max(scores, axis=-1, keepdims=True))
            probs = expo / jnp.sum(expo, axis=-1, keepdims=True)
            high_ref[:, at_probs + head * count : at_probs + (head + 1) * count] = probs
            outs.append(matmul(probs.astype(BF), values))
        attended.append(pick_heads(*outs).astype(BF))
    attended = matmul(jnp.concatenate(attended, axis=1), shuffle).astype(BF)
    low_ref[:, 4 * width : 5 * width] = attended
    at = near.shape[1] - width
    first = inputs + matmul(attended[:, :half], near[:, at:])
    first = first + matmul(attended[:, half:], far[:, at:])
    high_ref[:, :width] = first
    second = (first * inverse_rms(first) * gain_second).astype(BF)
    low_ref[:, 5 * width :] = second
    send(0)
    logits = nt(second, small[:LANES])
    lane = lax.broadcasted_iota(jnp.int32, logits.shape, 1)
    chosen = [
        jnp.sum(jnp.where(lane == routes[:, c : c + 1], logits, 0.0), axis=-1, keepdims=True)
        for c in range(2)
    ]
    top = jnp.maximum(chosen[0], chosen[1])
    expo = [jnp.exp(value - top) for value in chosen]
    gates = [value / (expo[0] + expo[1]) for value in expo]
    high_ref[:, width:at_probs] = jnp.where(lane == 0, gates[0], jnp.where(lane == 1, gates[1], 0.0))
    send(1)
    slot = lax.broadcasted_iota(jnp.int32, (outgoing_ref.shape[0], count), 0)
    rows = jnp.zeros(outgoing_ref.shape, F32)
    for c in range(2):
        hot = (slot == target_rows[c : c + 1]).astype(BF)
        rows = rows + matmul(hot, jnp.concatenate([second, lanes_of(gates[c], 0)], axis=1))
    outgoing_ref[...] = rows.astype(BF)


def expert_forward(rows, up):
    inner = nt(rows, up)
    square = inner * inner
    bend = jnp.tanh(0.7978845608028654 * inner * (1.0 + 0.044715 * square))
    slope = 0.5 * (1.0 + bend) + 0.5 * inner * (1.0 - bend * bend) * (
        0.7978845608028654 * (1.0 + 0.134145 * square)
    )
    return (0.5 * inner * (1.0 + bend)).astype(BF), slope


def gate_of(packed, width):
    return packed[:, width : width + 1].astype(F32) + packed[:, width + 1 : width + 2].astype(F32)


def expert_kernel(chips, column, *refs):
    rows, grads, refs = refs[:2], refs[2:4], refs[4:]
    weights, downs, refs = refs[:chips], refs[chips : 2 * chips], refs[2 * chips :]
    row_refs, kept_ref, shown_ref = refs[:2], refs[2], refs[3]
    count, width = grads[0].shape
    hidden = (weights[0].shape[0] + downs[0].shape[0]) // 2
    late = hidden - downs[0].shape[0]
    for core in range(2):
        packed, grad = rows[core], grads[core][...]
        gate = gate_of(packed, width)
        block = slice(core * count, (core + 1) * count)
        result, row_grad = jnp.zeros((count, width), F32), jnp.zeros((count, width), F32)
        for i in range(chips):
            up, down = weights[i][:hidden], (weights[i][hidden:], downs[i][...])
            active, slope = expert_forward(packed[:, :width], up)
            inner_grad = jnp.concatenate([nt(grad, part) for part in down], axis=1) * slope
            if i == 0:
                kept_ref[block, :hidden] = active
                kept_ref[block, hidden : 2 * hidden] = (inner_grad * gate).astype(BF)
            result = result + matmul(active[:, :late], down[0]) + matmul(active[:, late:], down[1])
            row_grad = row_grad + matmul(inner_grad.astype(BF), up)
        grad = grad.astype(F32)
        scaled = (grad * gate).astype(BF)
        kept_ref[block, 2 * hidden :] = scaled
        dots = jnp.sum(result * grad, axis=-1, keepdims=True)
        row_refs[core][...] = jnp.concatenate(
            [row_grad.astype(BF), lanes_of(dots, 2 * column[0, 0]), result.astype(BF)], axis=1
        )
    shown_ref[:count] = packed[:, :width]
    shown_ref[count:] = scaled


def weight_grad_kernel(weights, down_late, kept, far, near, *refs):
    others, (up_ref, down_ref) = refs[:-2], refs[-2:]
    width, hidden = up_ref.shape
    count = near.shape[0]
    up, down = weights[:hidden], (weights[hidden:], down_late[...])
    for i, rows in enumerate((far, near)):
        block = slice(i * count, (i + 1) * count)
        scaled = kept[block, 2 * hidden :]
        parts = (
            tn(rows[:, :width], kept[block, hidden : 2 * hidden]),
            tn(kept[block, :hidden], scaled),
        )
        if i == 0:
            up_ref[...], down_ref[...] = parts
        else:
            up_ref[...] += parts[0]
            down_ref[...] += parts[1]
    for ref in others:
        rows, scaled = ref[:count], ref[count:]
        active, slope = expert_forward(rows, up)
        inner_grad = jnp.concatenate([nt(scaled, part) for part in down], axis=1)
        up_ref[...] += tn(rows, (inner_grad * slope).astype(BF))
        down_ref[...] += tn(active, scaled)


def table_lanes(share):
    return BUCKETS * HEADS // share


def home_kernel(
    experts,
    share,
    home,
    routes,
    target,
    cotangent,
    place_of,
    low,
    high,
    near,
    far,
    flip_hot,
    keep_ref,
    send_ref,
    first_grad_ref,
    joint_grad_ref,
    distance_ref,
):
    count, width = cotangent.shape
    half = width // 2
    shuffle = shuffle_of(place_of)
    small_rows = small_of(small_lanes(experts), near, far, shuffle)
    at_probs = width + LANES
    slot = lax.broadcasted_iota(jnp.int32, (count, home.shape[0]), 1)
    lane = lax.broadcasted_iota(jnp.int32, (count, LANES), 1)
    gates = [high[:, width + c : width + c + 1] for c in range(2)]
    back = home[:, : width + LANES]
    routed = [matmul((slot == target[:, c : c + 1]).astype(BF), back) for c in range(2)]
    dots = [jnp.sum(value[:, width:], axis=-1, keepdims=True) for value in routed]
    mean = gates[0] * dots[0] + gates[1] * dots[1]
    logit_grad = jnp.zeros((count, LANES), F32)
    for c in range(2):
        logit_grad = jnp.where(lane == routes[:, c : c + 1], gates[c] * (dots[c] - mean), logit_grad)
    logit_grad = logit_grad.astype(BF)
    second_grad = gates[0] * routed[0][:, :width] + gates[1] * routed[1][:, :width]
    second_grad = second_grad + matmul(logit_grad, small_rows[:LANES])
    gain = small_rows[experts + 1 : experts + 2].astype(F32)
    first = high[:, :width]
    inverse = inverse_rms(first)
    unit = first * inverse
    scaled = second_grad * gain
    first_grad = cotangent[...].astype(F32) + inverse * (
        scaled - unit * jnp.mean(unit * scaled, axis=-1, keepdims=True)
    )
    first_grad_ref[...] = first_grad
    first_low = first_grad.astype(BF)
    attended_grad = jnp.concatenate(
        [nt(first_low, part[:, part.shape[1] - width :]) for part in (near, far)], axis=1
    ).astype(BF)
    attended_grad = nt(attended_grad, shuffle).astype(BF)
    value_grad = []
    for number in range(width // LANES):
        outs = [
            tn(
                high[:, at_probs + head * count : at_probs + (head + 1) * count].astype(BF),
                pair_of(attended_grad, number),
            )
            for head in (2 * number, 2 * number + 1)
        ]
        value_grad.append(pick_heads(*outs).astype(BF))
    value_grad = jnp.concatenate(value_grad, axis=1)
    joint_grad_ref[:, 2 * width :] = value_grad
    gain_part = second_grad * unit
    gain_high = gain_part.astype(BF)
    gain_rest = (gain_part - gain_high.astype(F32)).astype(BF)
    ones = (lane == experts).astype(BF)
    left = jnp.concatenate([low[:, 5 * width :], gain_high, gain_rest], axis=0)
    left = matmul(left, shuffle).astype(BF)
    right = jnp.concatenate([logit_grad, ones, ones], axis=0)
    small = tn(left, right)
    row = lax.broadcasted_iota(jnp.int32, (count, count), 0)
    for number in range(width // LANES):
        span = slice(number * LANES, (number + 1) * LANES)
        query, keys, values = (
            low[:, i * width + number * LANES : i * width + (number + 1) * LANES] for i in range(3)
        )
        own_grad = attended_grad[:, span]
        query_grads, key_grads = [], []
        for side in range(2):
            head = 2 * number + side
            chance = high[:, at_probs + head * count : at_probs + (head + 1) * count]
            prob_grad = nt(one_head(own_grad, side), values)
            score_grad = chance * (prob_grad - jnp.sum(chance * prob_grad, axis=-1, keepdims=True))
            lined = score_grad
            step = 1
            while step < count:
                lined = jnp.where((row // step) % 2 == 1, pltpu.roll(lined, count - step, 1), lined)
                step *= 2
            distance_ref[head : head + 1] = jnp.sum(lined, axis=0, keepdims=True)
            pair_grad = (score_grad * 0.125).astype(BF)
            query_grads.append(matmul(pair_grad, keys))
            key_grads.append(tn(pair_grad, query))
        joint_grad_ref[:, span] = pick_heads(*query_grads).astype(BF)
        joint_grad_ref[:, width + number * LANES : width + (number + 1) * LANES] = pick_heads(
            *key_grads
        ).astype(BF)
    table = jnp.dot(
        distance_ref[...], flip_hot[...], precision=lax.Precision.HIGHEST, preferred_element_type=F32
    ).astype(BF)
    lanes = table_lanes(share)
    spread = keep_ref.shape[1] - 4 * width
    value_row = lax.broadcasted_iota(jnp.int32, (width, HEADS), 0) % share * lanes
    value_head = lax.broadcasted_iota(jnp.int32, (width, HEADS), 1)
    bucket = lax.broadcasted_iota(jnp.int32, (BUCKETS, spread), 0)
    lane = lax.broadcasted_iota(jnp.int32, (BUCKETS, spread), 1) - (experts + 1)
    small = jnp.pad(small, ((0, 0), (0, spread - LANES)))
    for start in range(0, max(lanes, BUCKETS), min(lanes, BUCKETS)):
        if lanes <= BUCKETS:
            picked = (value_row == value_head * BUCKETS + start).astype(BF)
            put = ((lane >= 0) & (lane < lanes) & (bucket == lane + start)).astype(BF)
        else:
            picked = (value_row + start == value_head * BUCKETS).astype(BF)
            put = (lane - start == bucket).astype(BF)
        small = small + matmul(picked, matmul(table, put).astype(BF))
    joint_grads = joint_grad_ref[...]
    for ref, at in ((keep_ref, 0), (send_ref, half)):
        attended, normed = (low[:, i * width + at : i * width + at + half] for i in (4, 3))
        ref[:, : 3 * width] = tn(normed, joint_grads).astype(BF)
        ref[:, 3 * width : 4 * width] = tn(attended, first_low).astype(BF)
        ref[:, 4 * width :] = small[at : at + half].astype(BF)


def token_kernel(
    experts,
    tokens,
    first_grad,
    joint_grad,
    near,
    far,
    place_of,
    returned,
    target,
    high,
    token_ref,
    mixed_ref,
):
    count, width = tokens.shape
    slot = lax.broadcasted_iota(jnp.int32, (count, returned.shape[0]), 1)
    mixed = high[:, :width]
    for c in range(2):
        gate = high[:, width + c : width + c + 1]
        mixed = mixed + gate * matmul((slot == target[:, c : c + 1]).astype(BF), returned[...])
    mixed_ref[...] = mixed.astype(BF)
    shuffle = shuffle_of(place_of)
    gain = small_of(small_lanes(experts), near, far, shuffle)[experts : experts + 1].astype(F32)
    grads = joint_grad[...]
    normed_grad = jnp.concatenate(
        [nt(grads, part[:, : 3 * width]) for part in (near, far)], axis=1
    )
    large = normed_grad.astype(BF)
    rest = (normed_grad - large.astype(F32)).astype(BF)
    scaled = (nt(large, shuffle) + nt(rest, shuffle)) * gain
    inputs = tokens[...].astype(F32)
    inverse = inverse_rms(inputs)
    unit = inputs * inverse
    input_grad = inverse * (scaled - unit * jnp.mean(unit * scaled, axis=-1, keepdims=True))
    token_ref[...] = (first_grad[...] + input_grad).astype(BF)


def finish_kernel(experts, project_in, gain, *refs):
    parts, refs = refs[:-6], refs[-6:]
    grad_in_ref, sum_out_ref, router_ref, first_gain_ref, second_gain_ref, table_ref = refs
    sums = sum(part[...].astype(F32) for part in parts)
    share, width = sum_out_ref.shape
    grad_in = sums[:, : 3 * width]
    grad_in_ref[...] = grad_in
    sum_out_ref[...] = sums[:, 3 * width : 4 * width]
    small = sums[:, 4 * width :]
    router_ref[...] = small[:, :experts]
    row = lax.broadcasted_iota(jnp.int32, (share, share), 0)
    same = row == lax.broadcasted_iota(jnp.int32, (share, share), 1)

    def lined(column):
        return jnp.sum(jnp.where(same, column, 0.0), axis=0, keepdims=True)

    second_gain_ref[...] = lined(small[:, experts : experts + 1])
    grads = jnp.sum(grad_in * project_in[...].astype(F32), axis=-1, keepdims=True)
    first_gain_ref[...] = lined(grads) / gain[...].astype(F32)
    lanes = table_lanes(share)
    table = small[:, experts + 1 : experts + 1 + lanes]
    value_row = lax.broadcasted_iota(jnp.int32, (share, HEADS), 0) * lanes
    value_head = lax.broadcasted_iota(jnp.int32, (share, HEADS), 1)
    step = min(lanes, BUCKETS)
    total = jnp.zeros((BUCKETS, HEADS), F32)
    for start in range(0, max(lanes, BUCKETS), step):
        if lanes <= BUCKETS:
            picked, part = value_row == value_head * BUCKETS + start, table
        else:
            picked = value_row + start == value_head * BUCKETS
            part = table[:, start : start + step]
        put = lax.dot_general(
            part,
            picked.astype(F32),
            (((0,), (0,)), ((), ())),
            precision=lax.Precision.HIGHEST,
            preferred_element_type=F32,
        )
        if lanes <= BUCKETS:
            table_ref[start : start + step] = put
        else:
            total = total + put
            table_ref[...] = total


def on_device(
    tokens,
    cotangent,
    project_in,
    project_out,
    router,
    first_gain,
    second_gain,
    bias_table,
    expert_up,
    expert_down,
    positions,
    buckets,
    routes,
    slots,
):
    highest = lax.Precision.HIGHEST
    count, width = tokens.shape
    experts = lax.axis_size("expert")
    capacity = 3 * count // experts
    rows_here = experts * capacity
    share = project_in.shape[0]
    column = lax.axis_index("fsdp")
    mine = column * experts + lax.axis_index("expert")
    target = routes * capacity + slots
    slot_index = jnp.arange(rows_here, dtype=jnp.int32)
    hot = (slot_index[None, None, :] == jnp.transpose(target)[:, :, None]).astype(BF)
    place_hot = hot[0] + hot[1]
    grad_rows = contract_rows(place_hot, cotangent).astype(BF)
    grad_own = exchange(grad_rows)

    lanes = small_lanes(experts)
    hidden = expert_down.shape[1]
    late = hidden - hidden // 3
    packed, down_own = kernel_call(
        pack_kernel,
        [((share, lanes + 4 * width), BF), ((hidden - late, width), BF)],
        0,
        router.T,
        first_gain[None],
        second_gain[None],
        project_in,
        project_out,
        expert_down,
        fetch=(*range(5), (5, (0, slice(late, hidden)), (hidden - late, width))),
        scratch=56,
    )
    weights = stack([expert_up[0].T, expert_down[0, :late]])
    downs = fan(down_own, chip_masks())
    halves = gather_blocks(packed, (weights, *downs[1:]), (grad_own,))
    grad_parts = (grad_own, swap(grad_own, core_mask()))
    weights = fan(after(weights, halves[0]), chip_masks())
    feature = jnp.arange(width, dtype=jnp.int32)
    masks = jnp.asarray(np.repeat(np.array(block_masks(), np.int32), share))
    place_of = (masks ^ mine) * share + feature % share


    places = jnp.arange(count, dtype=jnp.int32)
    bucket_hot = (buckets[:, None] == jnp.arange(BUCKETS, dtype=jnp.int32)).astype(F32)
    flip = ((places[:, None] + places[None, :]) % count == 0).astype(F32)
    flip_hot = jnp.dot(flip, bucket_hot, precision=highest)
    bias_rows = lax.dot_general(
        bias_table, flip_hot, (((0,), (1,)), ((), ())), precision=highest
    )
    low, high, outgoing = kernel_call(
        functools.partial(forward_kernel, experts),
        [
            ((count, 6 * width), BF),
            ((count, width + LANES + HEADS * count), F32),
            ((rows_here, width + LANES), BF),
        ],
        2 * count * width * 6 * width,
        tokens,
        place_of[None],
        *halves,
        bias_rows,
        positions[:, None],
        routes,
        jnp.transpose(target),
        fetch=(0, 2, 3, 1, 4, 5, 6, 7),
        push=(0, 1, 2),
        scratch=56,
    )
    row_own = exchange(outgoing)
    row_parts = (row_own, swap(row_own, core_mask()))

    chips = len(chip_masks())
    piece = expert_up.shape[2]
    wide = (rows_here, 2 * width + LANES)
    row_far, row_near, kept, shown = kernel_call(
        functools.partial(expert_kernel, chips),
        [
            (wide, BF),
            (wide, BF),
            ((2 * rows_here, 2 * piece + width), BF),
            ((2 * rows_here, width), BF),
        ],
        16 * rows_here * width * chips * piece,
        column.astype(jnp.int32).reshape(1, 1),
        row_parts[1],
        row_parts[0],
        grad_parts[1],
        grad_parts[0],
        *weights,
        *downs,
        fetch=range(5, 5 + 2 * chips),
        scratch=56,
    )
    others = [swap(shown, mask) for mask in chip_masks()[1:]]
    others = [both for part in others for both in (part, swap(part, core_mask()))]
    (row_sum,) = sum_apart([row_near, swap(row_far, core_mask())], 1)
    home = after(exchange(row_sum), *others)

    half = width // 2
    table_at = experts + 1
    spread_lanes = -(-(table_at + table_lanes(share)) // LANES) * LANES
    keep, send, first_grad, joint_grad, _ = kernel_call(
        functools.partial(home_kernel, experts, share),
        [
            ((half, 4 * width + spread_lanes), BF),
            ((half, 4 * width + spread_lanes), BF),
            ((count, width), F32),
            ((count, 3 * width), BF),
            ((HEADS, count), F32),
        ],
        2 * count * width * 10 * width,
        home,
        routes,
        target,
        cotangent,
        place_of[None],
        low,
        high,
        *halves,
        flip_hot,
        fetch=(
            6,
            (7, (slice(None), slice(3 * width, None)), (half, lanes + width)),
            (8, (slice(None), slice(3 * width, None)), (half, lanes + width)),
            3,
            5,
        ),
        scratch=56,
    )
    def meanwhile(begun):
        grad_up, grad_down = kernel_call(
            weight_grad_kernel,
            [((width, piece), F32), ((piece, width), F32)],
            16 * rows_here * width * chips * piece,
            weights[0],
            down_own,
            after(kept, begun),
            row_parts[1],
            row_parts[0],
            *others,
            fetch=range(5 + len(others)),
            scratch=56,
        )
        token_grad, mixed = kernel_call(
            functools.partial(token_kernel, experts),
            [((count, width), BF), ((count, width), BF)],
            2 * count * width * 6 * width,
            tokens,
            first_grad,
            after(joint_grad, begun),
            *halves,
            place_of[None],
            home,
            target,
            high,
            fetch=(
                (6, (slice(None), slice(width + LANES, None)), (rows_here, width)),
                (8, (slice(None), slice(0, width + LANES)), (count, width + LANES)),
                3,
                4,
                0,
                1,
                2,
            ),
            scratch=56,
        )
        return grad_up, grad_down, token_grad, mixed

    blocks, done = scatter_blocks(keep, send, meanwhile)
    grad_up, grad_down, token_grad, mixed = done
    grad_in, sum_out, grad_router, grad_first_gain, grad_second_gain, table_total = kernel_call(
        functools.partial(finish_kernel, experts),
        [
            ((share, 3 * width), F32),
            ((share, width), F32),
            ((share, experts), F32),
            ((1, share), F32),
            ((1, share), F32),
            ((BUCKETS, HEADS), F32),
        ],
        share * width * 8,
        project_in,
        first_gain[None],
        *blocks,
    )
    return (
        mixed,
        token_grad,
        grad_in,
        sum_out,
        grad_router,
        grad_first_gain[0],
        grad_second_gain[0],
        table_total,
        grad_up[None],
        grad_down[None],
    )


def solution(mesh):
    rows = P(("fsdp", "expert"), None)
    line = P(("fsdp", "expert"))
    up, down = P("expert", None, "fsdp"), P("expert", "fsdp", None)
    return jax.shard_map(
        on_device,
        mesh=mesh,
        in_specs=(rows, rows, rows, rows, rows, line, line, P(), up, down, line, P(), rows, rows),
        out_specs=(rows, rows, rows, rows, rows, line, line, P(), up, down),
        check_vma=False,
    )
```

```python
import functools
import math

import jax
import jax.numpy as jnp
import numpy as np
from jax import lax
from jax.experimental import pallas as pl
from jax.experimental.pallas import tpu as pltpu
from jax.sharding import PartitionSpec as P

HEADS = 12
HEAD = 64
BUCKETS = 32
LANES = 128
BF = jnp.bfloat16
F32 = jnp.float32


def rms_scale(value, gain):
    return value * lax.rsqrt(jnp.mean(value * value, axis=-1, keepdims=True) + 1e-06) * gain


def contract_rows(left, right):
    return lax.dot_general(left, right, (((0,), (0,)), ((), ())), preferred_element_type=F32)


def contract_cols(left, right):
    return lax.dot_general(left, right, (((1,), (1,)), ((), ())), preferred_element_type=F32)


def matmul(left, right):
    return jnp.dot(left, right, preferred_element_type=F32)


AXES = ("fsdp", "expert")


def sizes():
    return lax.axis_size("fsdp"), lax.axis_size("expert")


def core_mask():
    return sizes()[1]


def xy_masks():
    columns, experts = sizes()
    return [2 * experts * x + y for y in range(2) for x in range(columns // 2)]


def chip_masks():
    columns, experts = sizes()
    return [2 * experts * x for x in range(columns // 2)]


def z_bits():
    experts = sizes()[1]
    return [1 << bit for bit in range(1, experts.bit_length() - 1)]


def chip_bits():
    columns, experts = sizes()
    return [experts << bit for bit in range(1, columns.bit_length() - 1)]


def z_masks():
    order = [0]
    for mask in reversed(z_bits()):
        order = order + [k + mask for k in order]
    return order


def block_masks():
    return [c + xy + z for c in (0, core_mask()) for xy in xy_masks() for z in z_masks()]


def swap(value, mask):
    columns, experts = sizes()
    return lax.ppermute(value, AXES, [(i, i ^ mask) for i in range(columns * experts)])


def tied(value, other):
    return lax.optimization_barrier((value, other))[0]


def fan(value, masks):
    return [value] + [swap(value, mask) for mask in masks[1:]]


def stack(parts):
    return jnp.concatenate(parts, axis=0)


def after(value, *others):
    return pl.pallas_call(
        lambda *refs: None,
        out_shape=jax.ShapeDtypeStruct(value.shape, value.dtype),
        in_specs=[pl.BlockSpec(memory_space=pl.ANY)] * (1 + len(others)),
        out_specs=pl.BlockSpec(memory_space=pl.ANY),
        input_output_aliases={0: 0},
    )(value, *others)


def gather_blocks(value, early, late):
    value = stack(fan(value, z_masks()))
    value = after(stack(fan(after(value, *early), xy_masks())), *late)
    return value, swap(value, core_mask())


def add_low(own, arrived):
    return (own.astype(F32) + arrived.astype(F32)).astype(BF)


def sum_of(refs):
    return sum((ref[...].astype(F32) for ref in refs[1:]), refs[0][...].astype(F32))


def sum_kernel(inputs, *refs):
    total = sum_of(refs[:inputs])
    rows = total.shape[0] // (len(refs) - inputs)
    for i, ref in enumerate(refs[inputs:]):
        ref[...] = total[i * rows : (i + 1) * rows].astype(BF)


def sum_apart(parts, pieces):
    rows, width = parts[0].shape
    outs = [((rows // pieces, width), BF)] * pieces
    return kernel_call(functools.partial(sum_kernel, len(parts)), outs, rows * width, *parts)


def halves_of(total, rows):
    runs = [total[at : at + rows].astype(BF) for at in range(0, total.shape[0], rows)]
    return jnp.concatenate(runs[::2], axis=0), jnp.concatenate(runs[1::2], axis=0)


def halve_kernel(rows, own, arrived, keep_ref, send_ref):
    keep_ref[...], send_ref[...] = halves_of(sum_of((own, arrived)), rows)


def halve(own, arrived, rows):
    outs = [((own.shape[0] // 2, own.shape[1]), BF)] * 2
    return kernel_call(functools.partial(halve_kernel, rows), outs, own.size, own, arrived)


def begin_kernel(cut, rows, own, arrived, *refs):
    total = sum_of((own, arrived))
    *leads, keep_ref, send_ref = refs
    count = total.shape[0] // len(leads)
    for i, ref in enumerate(leads):
        ref[...] = total[i * count : (i + 1) * count, :cut].astype(BF)
    keep_ref[...], send_ref[...] = halves_of(total[:, cut:], rows)


def scatter_blocks(value, other, first, second):
    xy, z = xy_masks(), z_masks()
    count, width = value.shape
    share = count // (len(xy) * len(z))
    cut = 3 * (width // LANES) // 4 * LANES
    bits = z_bits()
    steps = [(mask, share << (len(bits) - 1 - i)) for i, mask in enumerate(bits)]
    bits = [1, *reversed(chip_bits())]
    steps += [(mask, share << (len(bits) - 1 - i)) for i, mask in enumerate(bits)]
    *leads, keep, send = kernel_call(
        functools.partial(begin_kernel, cut, steps[0][1]),
        [((count // len(xy), cut), BF)] * len(xy) + [((count // 2, width - cut), BF)] * 2,
        value.size,
        value,
        swap(other, core_mask()),
    )
    arrived = fan_sends(leads, xy)
    done = first(leads[0])
    for i, (mask, _) in enumerate(steps):
        if i == len(z_bits()):
            keep = after(keep, sums[0])
        come = swap(send, mask)
        if i == 1:
            come = after(come, *done)
        if i + 1 == len(steps):
            break
        keep, send = halve(keep, come, steps[i + 1][1])
        if i == 0:
            sums = sum_apart([leads[0], *arrived], len(z))
    later = second(sums[0])
    return [sums[0], *fan_sends(sums, z)], [after(keep, *later), come], done, later


def fan_sends(parts, masks):
    return [swap(part, mask) for part, mask in zip(parts[1:], masks[1:])]


def exchange(value):
    experts = lax.axis_size("expert")
    blocks = value.reshape(experts, value.shape[0] // experts, value.shape[1])
    moved = lax.all_to_all(blocks, "expert", split_axis=0, concat_axis=0, tiled=True)
    return moved.reshape(value.shape)


def lanes_of(value, place):
    high = value.astype(BF)
    rest = (value - high.astype(F32)).astype(BF)
    lane = lax.broadcasted_iota(jnp.int32, (value.shape[0], LANES), 1)
    nothing = jnp.zeros((), BF)
    return jnp.where(lane == place, high, jnp.where(lane == place + 1, rest, nothing))


def nt(left, right):
    return contract_cols(left, right)


def tn(left, right):
    return contract_rows(left, right)


class Incoming:
    def __init__(self, ref, copy):
        self.ref, self.copy = ref, copy
        self.shape, self.dtype = ref.shape, ref.dtype
        copy.start()

    def wait(self):
        if self.copy is not None:
            self.copy.wait()
            self.copy = None

    def __getitem__(self, index):
        self.wait()
        return self.ref[index]


def kernel_call(body, outs, flops, *operands, fetch=(), push=(), scratch=16):
    moved = sum(math.prod(v.shape) * v.dtype.itemsize for v in operands)
    moved += sum(math.prod(shape) * jnp.dtype(kind).itemsize for shape, kind in outs)
    taken = len(operands)
    fetch = [
        item if isinstance(item, tuple) else (item, ..., operands[item].shape) for item in fetch
    ]
    push = list(push)

    def kernel(*refs):
        buffers, refs = refs[taken + len(outs) :], list(refs[: taken + len(outs)])
        arriving, leaving, sent = [], {}, []
        for i, (number, index, _) in enumerate(fetch):
            source = refs[number] if index is ... else refs[number].at[index]
            copy = pltpu.make_async_copy(source, buffers[i], buffers[-1].at[i])
            refs[number] = Incoming(buffers[i], copy)
            arriving.append(refs[number])
        for i, number in enumerate(push, len(fetch)):
            leaving[number] = pltpu.make_async_copy(
                buffers[i], refs[taken + number], buffers[-1].at[i]
            )
            refs[taken + number] = buffers[i]

        def send(number):
            leaving[number].start()
            sent.append(number)

        body(*refs, *([send] if push else []))
        for number in push:
            if number not in sent:
                send(number)
        for value in arriving:
            value.wait()
        for number in push:
            leaving[number].wait()

    whole, left = pl.BlockSpec(memory_space=pltpu.VMEM), pl.BlockSpec(memory_space=pl.ANY)
    fetched = [number for number, _, _ in fetch]
    buffers = [pltpu.VMEM(shape, operands[number].dtype) for number, _, shape in fetch]
    buffers += [pltpu.VMEM(*outs[number]) for number in push]
    if buffers:
        buffers.append(pltpu.SemaphoreType.DMA((len(buffers),)))
    return pl.pallas_call(
        kernel,
        out_shape=[jax.ShapeDtypeStruct(shape, kind) for shape, kind in outs],
        in_specs=[left if i in fetched else whole for i in range(taken)],
        out_specs=[left if i in push else whole for i in range(len(outs))],
        scratch_shapes=buffers,
        compiler_params=pltpu.CompilerParams(vmem_limit_bytes=scratch * 1024 * 1024),
        cost_estimate=pl.CostEstimate(flops=0, bytes_accessed=0, transcendentals=0),
    )(*operands)


def pick_heads(first_head, second_head):
    lane = lax.broadcasted_iota(jnp.int32, first_head.shape, 1)
    return jnp.where(lane < HEAD, first_head, second_head)


def one_head(pair, side):
    lane = lax.broadcasted_iota(jnp.int32, pair.shape, 1)
    return jnp.where((lane < HEAD) == (side == 0), pair, jnp.zeros((), pair.dtype))


def pair_of(value, number):
    return value[:, number * LANES : (number + 1) * LANES]


def inverse_rms(value):
    return lax.rsqrt(jnp.mean(value * value, axis=-1, keepdims=True) + 1e-06)


def small_lanes(experts):
    return -(-(experts + 2) // LANES) * LANES


def shuffle_of(place_of):
    width = place_of.shape[1]
    return (lax.broadcasted_iota(jnp.int32, (width, width), 0) == place_of[...]).astype(BF)


def small_of(lanes, near, far, shuffle):
    end = near.shape[1] - shuffle.shape[0]
    start = end - lanes
    rows = jnp.concatenate([near[:, start:end], far[:, start:end]], axis=0)
    return jnp.transpose(matmul(shuffle, rows)).astype(BF)


def pack_kernel(
    router_rows, first_gain, second_gain, project_in, project_out, down, packed_ref, down_ref
):
    share, columns = project_in.shape
    experts = router_rows.shape[0]
    lanes = packed_ref.shape[1] - columns - project_out.shape[1]
    eye = lax.broadcasted_iota(jnp.int32, (share, share), 0)
    eye = (eye == lax.broadcasted_iota(jnp.int32, (share, share), 1)).astype(BF)
    rows = jnp.concatenate(
        [router_rows[...], first_gain[...], second_gain[...], jnp.zeros((lanes - experts - 2, share), BF)],
        axis=0,
    )
    packed_ref[:, :columns] = project_in[...]
    packed_ref[:, columns : columns + lanes] = nt(eye, rows).astype(BF)
    packed_ref[:, columns + lanes :] = project_out[...]
    down_ref[...] = down[...]


def forward_kernel(
    experts,
    tokens,
    place_of,
    near,
    far,
    bias_rows,
    positions,
    routes,
    target_rows,
    low_ref,
    high_ref,
    outgoing_ref,
    send,
):
    count, width = tokens.shape
    at_probs = width + LANES
    shuffle = shuffle_of(place_of)
    small = small_of(small_lanes(experts), near, far, shuffle)
    half = width // 2
    inputs = tokens[...].astype(F32)
    gain_first = small[experts : experts + 1].astype(F32)
    gain_second = small[experts + 1 : experts + 2].astype(F32)
    normed = (inputs * inverse_rms(inputs) * gain_first).astype(BF)
    normed = matmul(normed, shuffle).astype(BF)
    low_ref[:, 3 * width : 4 * width] = normed
    joint = matmul(normed[:, :half], near[:, : 3 * width])
    joint = joint + matmul(normed[:, half:], far[:, : 3 * width])
    low_ref[:, : 3 * width] = joint.astype(BF)
    row = lax.broadcasted_iota(jnp.int32, (count, count), 0)
    distance = row - lax.broadcasted_iota(jnp.int32, (count, count), 1)
    valid = (distance >= 0) & (distance <= positions[...])
    pairs = width // LANES
    attended = []
    for number in range(pairs):
        query, keys, values = (
            low_ref[:, i * width + number * LANES : i * width + (number + 1) * LANES] for i in range(3)
        )
        outs = []
        for side in range(2):
            head = 2 * number + side
            bias = jnp.broadcast_to(bias_rows[head : head + 1], (count, count))
            bias = pltpu.roll(bias, 0, 1, stride=1, stride_axis=0)
            scores = jnp.where(valid, nt(one_head(query, side), keys) * 0.125 + bias, -1e30)
            expo = jnp.exp(scores - jnp.max(scores, axis=-1, keepdims=True))
            probs = expo / jnp.sum(expo, axis=-1, keepdims=True)
            high_ref[:, at_probs + head * count : at_probs + (head + 1) * count] = probs
            outs.append(matmul(probs.astype(BF), values))
        attended.append(pick_heads(*outs).astype(BF))
    attended = matmul(jnp.concatenate(attended, axis=1), shuffle).astype(BF)
    low_ref[:, 4 * width : 5 * width] = attended
    at = near.shape[1] - width
    first = inputs + matmul(attended[:, :half], near[:, at:])
    first = first + matmul(attended[:, half:], far[:, at:])
    high_ref[:, :width] = first
    second = (first * inverse_rms(first) * gain_second).astype(BF)
    low_ref[:, 5 * width :] = second
    send(0)
    logits = nt(second, small[:LANES])
    lane = lax.broadcasted_iota(jnp.int32, logits.shape, 1)
    chosen = [
        jnp.sum(jnp.where(lane == routes[:, c : c + 1], logits, 0.0), axis=-1, keepdims=True)
        for c in range(2)
    ]
    top = jnp.maximum(chosen[0], chosen[1])
    expo = [jnp.exp(value - top) for value in chosen]
    gates = [value / (expo[0] + expo[1]) for value in expo]
    high_ref[:, width:at_probs] = jnp.where(lane == 0, gates[0], jnp.where(lane == 1, gates[1], 0.0))
    send(1)
    slot = lax.broadcasted_iota(jnp.int32, (outgoing_ref.shape[0], count), 0)
    rows = jnp.zeros(outgoing_ref.shape, F32)
    for c in range(2):
        hot = (slot == target_rows[c : c + 1]).astype(BF)
        rows = rows + matmul(hot, jnp.concatenate([second, lanes_of(gates[c], 0)], axis=1))
    outgoing_ref[...] = rows.astype(BF)


def expert_forward(rows, up):
    inner = nt(rows, up)
    square = inner * inner
    bend = jnp.tanh(0.7978845608028654 * inner * (1.0 + 0.044715 * square))
    slope = 0.5 * (1.0 + bend) + 0.5 * inner * (1.0 - bend * bend) * (
        0.7978845608028654 * (1.0 + 0.134145 * square)
    )
    return (0.5 * inner * (1.0 + bend)).astype(BF), slope


def gate_of(packed, width):
    return packed[:, width : width + 1].astype(F32) + packed[:, width + 1 : width + 2].astype(F32)


def expert_kernel(chips, *refs):
    rows, grads, refs = refs[:2], refs[2:4], refs[4:]
    weights, downs, refs = refs[:chips], refs[chips : 2 * chips], refs[2 * chips :]
    row_refs, kept_ref, shown_ref = refs[:2], refs[2], refs[3]
    count, width = grads[0].shape
    hidden = (weights[0].shape[0] + downs[0].shape[0]) // 2
    late = hidden - downs[0].shape[0]
    for core in range(2):
        packed, grad = rows[core], grads[core][...]
        gate = gate_of(packed, width)
        block = slice(core * count, (core + 1) * count)
        result, row_grad = jnp.zeros((count, width), F32), jnp.zeros((count, width), F32)
        for i in range(chips):
            up, down = weights[i][:hidden], (weights[i][hidden:], downs[i][...])
            active, slope = expert_forward(packed[:, :width], up)
            inner_grad = jnp.concatenate([nt(grad, part) for part in down], axis=1) * slope
            if i == 0:
                kept_ref[block, :hidden] = active
                kept_ref[block, hidden : 2 * hidden] = (inner_grad * gate).astype(BF)
            result = result + matmul(active[:, :late], down[0]) + matmul(active[:, late:], down[1])
            row_grad = row_grad + matmul(inner_grad.astype(BF), up)
        grad = grad.astype(F32)
        scaled = (grad * gate).astype(BF)
        kept_ref[block, 2 * hidden :] = scaled
        row_refs[core][:, :width] = row_grad.astype(BF)
        row_refs[core][:, width:] = result.astype(BF)
    shown_ref[:count] = packed[:, :width]
    shown_ref[count:] = scaled


def weight_grad_kernel(weights, down_late, kept, far, near, *refs):
    others, (up_ref, down_ref) = refs[:-2], refs[-2:]
    width, hidden = up_ref.shape
    count = near.shape[0]
    up, down = weights[:hidden], (weights[hidden:], down_late[...])
    rows = stack([far[:, :width], near[:, :width]])
    up_grad = tn(rows, kept[:, hidden : 2 * hidden])
    down_grad = tn(kept[:, :hidden], kept[:, 2 * hidden :])
    for pair in zip(others[::2], others[1::2]):
        rows = stack([part[:count] for part in pair])
        scaled = stack([part[count:] for part in pair])
        active, slope = expert_forward(rows, up)
        inner_grad = jnp.concatenate([nt(scaled, part) for part in down], axis=1)
        up_grad = up_grad + tn(rows, (inner_grad * slope).astype(BF))
        down_grad = down_grad + tn(active, scaled)
    up_ref[...] = up_grad
    down_ref[...] = down_grad


def table_lanes(share):
    return BUCKETS * HEADS // share


def home_kernel(
    experts,
    share,
    home,
    routes,
    target,
    cotangent,
    place_of,
    low,
    high,
    near,
    far,
    flip_hot,
    keep_ref,
    send_ref,
    first_grad_ref,
    joint_grad_ref,
    distance_ref,
    mixed_ref,
):
    count, width = cotangent.shape
    half = width // 2
    shuffle = shuffle_of(place_of)
    small_rows = small_of(small_lanes(experts), near, far, shuffle)
    at_probs = width + LANES
    slot = lax.broadcasted_iota(jnp.int32, (count, home.shape[0]), 1)
    lane = lax.broadcasted_iota(jnp.int32, (count, LANES), 1)
    gates = [high[:, width + c : width + c + 1] for c in range(2)]
    routed = [matmul((slot == target[:, c : c + 1]).astype(BF), home[...]) for c in range(2)]
    returned = [value[:, width:] for value in routed]
    upstream = cotangent[...].astype(F32)
    dots = [jnp.sum(upstream * value, axis=-1, keepdims=True) for value in returned]
    mean = gates[0] * dots[0] + gates[1] * dots[1]
    logit_grad = jnp.zeros((count, LANES), F32)
    for c in range(2):
        logit_grad = jnp.where(lane == routes[:, c : c + 1], gates[c] * (dots[c] - mean), logit_grad)
    logit_grad = logit_grad.astype(BF)
    second_grad = gates[0] * routed[0][:, :width] + gates[1] * routed[1][:, :width]
    second_grad = second_grad + matmul(logit_grad, small_rows[:LANES])
    gain = small_rows[experts + 1 : experts + 2].astype(F32)
    first = high[:, :width]
    mixed_ref[...] = (first + gates[0] * returned[0] + gates[1] * returned[1]).astype(BF)
    inverse = inverse_rms(first)
    unit = first * inverse
    scaled = second_grad * gain
    first_grad = upstream + inverse * (
        scaled - unit * jnp.mean(unit * scaled, axis=-1, keepdims=True)
    )
    first_grad_ref[...] = first_grad
    first_low = first_grad.astype(BF)
    attended_grad = jnp.concatenate(
        [nt(first_low, part[:, part.shape[1] - width :]) for part in (near, far)], axis=1
    ).astype(BF)
    attended_grad = nt(attended_grad, shuffle).astype(BF)
    value_grad = []
    for number in range(width // LANES):
        outs = [
            tn(
                high[:, at_probs + head * count : at_probs + (head + 1) * count].astype(BF),
                pair_of(attended_grad, number),
            )
            for head in (2 * number, 2 * number + 1)
        ]
        value_grad.append(pick_heads(*outs).astype(BF))
    value_grad = jnp.concatenate(value_grad, axis=1)
    joint_grad_ref[:, 2 * width :] = value_grad
    gain_part = second_grad * unit
    gain_high = gain_part.astype(BF)
    gain_rest = (gain_part - gain_high.astype(F32)).astype(BF)
    ones = (lane == experts).astype(BF)
    left = jnp.concatenate([low[:, 5 * width :], gain_high, gain_rest], axis=0)
    left = matmul(left, shuffle).astype(BF)
    right = jnp.concatenate([logit_grad, ones, ones], axis=0)
    small = tn(left, right)
    row = lax.broadcasted_iota(jnp.int32, (count, count), 0)
    for number in range(width // LANES):
        span = slice(number * LANES, (number + 1) * LANES)
        query, keys, values = (
            low[:, i * width + number * LANES : i * width + (number + 1) * LANES] for i in range(3)
        )
        own_grad = attended_grad[:, span]
        query_grads, key_grads = [], []
        for side in range(2):
            head = 2 * number + side
            chance = high[:, at_probs + head * count : at_probs + (head + 1) * count]
            prob_grad = nt(one_head(own_grad, side), values)
            score_grad = chance * (prob_grad - jnp.sum(chance * prob_grad, axis=-1, keepdims=True))
            lined = score_grad
            step = 1
            while step < count:
                lined = jnp.where((row // step) % 2 == 1, pltpu.roll(lined, count - step, 1), lined)
                step *= 2
            distance_ref[head : head + 1] = jnp.sum(lined, axis=0, keepdims=True)
            pair_grad = (score_grad * 0.125).astype(BF)
            query_grads.append(matmul(pair_grad, keys))
            key_grads.append(tn(pair_grad, query))
        joint_grad_ref[:, span] = pick_heads(*query_grads).astype(BF)
        joint_grad_ref[:, width + number * LANES : width + (number + 1) * LANES] = pick_heads(
            *key_grads
        ).astype(BF)
    table = jnp.dot(
        distance_ref[...], flip_hot[...], precision=lax.Precision.HIGHEST, preferred_element_type=F32
    ).astype(BF)
    lanes = table_lanes(share)
    spread = keep_ref.shape[1] - 4 * width
    value_row = lax.broadcasted_iota(jnp.int32, (width, HEADS), 0) % share * lanes
    value_head = lax.broadcasted_iota(jnp.int32, (width, HEADS), 1)
    bucket = lax.broadcasted_iota(jnp.int32, (BUCKETS, spread), 0)
    lane = lax.broadcasted_iota(jnp.int32, (BUCKETS, spread), 1) - (experts + 1)
    small = jnp.pad(small, ((0, 0), (0, spread - LANES)))
    for start in range(0, max(lanes, BUCKETS), min(lanes, BUCKETS)):
        if lanes <= BUCKETS:
            picked = (value_row == value_head * BUCKETS + start).astype(BF)
            put = ((lane >= 0) & (lane < lanes) & (bucket == lane + start)).astype(BF)
        else:
            picked = (value_row + start == value_head * BUCKETS).astype(BF)
            put = (lane - start == bucket).astype(BF)
        small = small + matmul(picked, matmul(table, put).astype(BF))
    joint_grads = joint_grad_ref[...]
    for ref, at in ((keep_ref, 0), (send_ref, half)):
        attended, normed = (low[:, i * width + at : i * width + at + half] for i in (4, 3))
        ref[:, : 3 * width] = tn(normed, joint_grads).astype(BF)
        ref[:, 3 * width : 4 * width] = tn(attended, first_low).astype(BF)
        ref[:, 4 * width :] = small[at : at + half].astype(BF)


def token_kernel(
    experts,
    tokens,
    first_grad,
    joint_grad,
    near,
    far,
    place_of,
    token_ref,
):
    width = tokens.shape[1]
    shuffle = shuffle_of(place_of)
    gain = small_of(small_lanes(experts), near, far, shuffle)[experts : experts + 1].astype(F32)
    grads = joint_grad[...]
    normed_grad = jnp.concatenate(
        [nt(grads, part[:, : 3 * width]) for part in (near, far)], axis=1
    )
    large = normed_grad.astype(BF)
    rest = (normed_grad - large.astype(F32)).astype(BF)
    scaled = (nt(large, shuffle) + nt(rest, shuffle)) * gain
    inputs = tokens[...].astype(F32)
    inverse = inverse_rms(inputs)
    unit = inputs * inverse
    input_grad = inverse * (scaled - unit * jnp.mean(unit * scaled, axis=-1, keepdims=True))
    token_ref[...] = (first_grad[...] + input_grad).astype(BF)


def finish_kernel(experts, leads, project_in, gain, *refs):
    parts, refs = refs[:-6], refs[-6:]
    grad_in_ref, sum_out_ref, router_ref, first_gain_ref, second_gain_ref, table_ref = refs
    sums = jnp.concatenate([sum_of(parts[:leads]), sum_of(parts[leads:])], axis=1)
    share, width = sum_out_ref.shape
    grad_in = sums[:, : 3 * width]
    grad_in_ref[...] = grad_in
    sum_out_ref[...] = sums[:, 3 * width : 4 * width]
    small = sums[:, 4 * width :]
    row = lax.broadcasted_iota(jnp.int32, (share, share), 0)
    same = row == lax.broadcasted_iota(jnp.int32, (share, share), 1)

    router_ref[...] = lax.dot_general(
        small[:, :experts],
        same.astype(F32),
        (((0,), (0,)), ((), ())),
        precision=lax.Precision.HIGHEST,
        preferred_element_type=F32,
    )

    def lined(column):
        return jnp.sum(jnp.where(same, column, 0.0), axis=0, keepdims=True)

    second_gain_ref[...] = lined(small[:, experts : experts + 1])
    grads = jnp.sum(grad_in * project_in[...].astype(F32), axis=-1, keepdims=True)
    first_gain_ref[...] = lined(grads) / gain[...].astype(F32)
    lanes = table_lanes(share)
    table = small[:, experts + 1 : experts + 1 + lanes]
    value_row = lax.broadcasted_iota(jnp.int32, (share, HEADS), 0) * lanes
    value_head = lax.broadcasted_iota(jnp.int32, (share, HEADS), 1)
    step = min(lanes, BUCKETS)
    total = jnp.zeros((HEADS, BUCKETS), F32)
    for start in range(0, max(lanes, BUCKETS), step):
        if lanes <= BUCKETS:
            picked, part = value_row == value_head * BUCKETS + start, table
        else:
            picked = value_row + start == value_head * BUCKETS
            part = table[:, start : start + step]
        put = lax.dot_general(
            picked.astype(F32),
            part,
            (((0,), (0,)), ((), ())),
            precision=lax.Precision.HIGHEST,
            preferred_element_type=F32,
        )
        if lanes <= BUCKETS:
            table_ref[:, start : start + step] = put
        else:
            total = total + put
            table_ref[...] = total


def on_device(
    tokens,
    cotangent,
    project_in,
    project_out,
    router,
    first_gain,
    second_gain,
    bias_table,
    expert_up,
    expert_down,
    positions,
    buckets,
    routes,
    slots,
):
    highest = lax.Precision.HIGHEST
    count, width = tokens.shape
    experts = lax.axis_size("expert")
    capacity = 3 * count // experts
    rows_here = experts * capacity
    share = project_in.shape[0]
    column = lax.axis_index("fsdp")
    mine = column * experts + lax.axis_index("expert")
    target = routes * capacity + slots
    slot_index = jnp.arange(rows_here, dtype=jnp.int32)
    hot = (slot_index[None, None, :] == jnp.transpose(target)[:, :, None]).astype(BF)
    place_hot = hot[0] + hot[1]
    grad_rows = contract_rows(place_hot, cotangent).astype(BF)
    grad_own = exchange(grad_rows)

    lanes = small_lanes(experts)
    hidden = expert_down.shape[1]
    late = hidden - hidden // 3
    packed, down_own = kernel_call(
        pack_kernel,
        [((share, lanes + 4 * width), BF), ((hidden - late, width), BF)],
        0,
        router.T,
        first_gain[None],
        second_gain[None],
        project_in,
        project_out,
        expert_down,
        fetch=(*range(5), (5, (0, slice(late, hidden)), (hidden - late, width))),
        scratch=56,
    )
    weights = stack([expert_up[0].T, expert_down[0, :late]])
    downs = fan(down_own, chip_masks())
    halves = gather_blocks(packed, (weights, *downs[1:]), (grad_own,))
    grad_parts = (grad_own, swap(grad_own, core_mask()))
    weights = fan(after(weights, halves[0]), chip_masks())
    feature = jnp.arange(width, dtype=jnp.int32)
    masks = jnp.asarray(np.repeat(np.array(block_masks(), np.int32), share))
    place_of = (masks ^ mine) * share + feature % share


    places = jnp.arange(count, dtype=jnp.int32)
    bucket_hot = (buckets[:, None] == jnp.arange(BUCKETS, dtype=jnp.int32)).astype(F32)
    flip = ((places[:, None] + places[None, :]) % count == 0).astype(F32)
    flip_hot = jnp.dot(flip, bucket_hot, precision=highest)
    bias_rows = lax.dot_general(
        bias_table, flip_hot, (((0,), (1,)), ((), ())), precision=highest
    )
    low, high, outgoing = kernel_call(
        functools.partial(forward_kernel, experts),
        [
            ((count, 6 * width), BF),
            ((count, width + LANES + HEADS * count), F32),
            ((rows_here, width + LANES), BF),
        ],
        2 * count * width * 6 * width,
        tokens,
        place_of[None],
        *halves,
        bias_rows,
        positions[:, None],
        routes,
        jnp.transpose(target),
        fetch=(0, 2, 3, 1, 4, 5, 6, 7),
        push=(0, 1, 2),
        scratch=56,
    )
    row_own = exchange(outgoing)
    row_parts = (row_own, swap(row_own, core_mask()))

    chips = len(chip_masks())
    piece = expert_up.shape[2]
    wide = (rows_here, 2 * width)
    row_far, row_near, kept, shown = kernel_call(
        functools.partial(expert_kernel, chips),
        [
            (wide, BF),
            (wide, BF),
            ((2 * rows_here, 2 * piece + width), BF),
            ((2 * rows_here, width), BF),
        ],
        16 * rows_here * width * chips * piece,
        row_parts[1],
        row_parts[0],
        grad_parts[1],
        grad_parts[0],
        *weights,
        *downs,
        fetch=range(4, 4 + 2 * chips),
        scratch=56,
    )
    others = [swap(shown, mask) for mask in chip_masks()[1:]]
    others = [both for part in others for both in (part, swap(part, core_mask()))]
    (row_sum,) = sum_apart([row_near, swap(row_far, core_mask())], 1)
    home = after(exchange(row_sum), *others)

    half = width // 2
    table_at = experts + 1
    spread_lanes = -(-(table_at + table_lanes(share)) // LANES) * LANES
    keep, send, first_grad, joint_grad, _, mixed = kernel_call(
        functools.partial(home_kernel, experts, share),
        [
            ((half, 4 * width + spread_lanes), BF),
            ((half, 4 * width + spread_lanes), BF),
            ((count, width), F32),
            ((count, 3 * width), BF),
            ((HEADS, count), F32),
            ((count, width), BF),
        ],
        2 * count * width * 10 * width,
        home,
        routes,
        target,
        cotangent,
        place_of[None],
        low,
        high,
        *halves,
        flip_hot,
        fetch=(
            6,
            (7, (slice(None), slice(3 * width, None)), (half, lanes + width)),
            (8, (slice(None), slice(3 * width, None)), (half, lanes + width)),
            3,
            5,
        ),
        scratch=56,
    )
    def token_parts(begun):
        return kernel_call(
            functools.partial(token_kernel, experts),
            [((count, width), BF)],
            2 * count * width * 6 * width,
            tokens,
            first_grad,
            after(joint_grad, begun),
            *halves,
            place_of[None],
            fetch=(3, 4, 0, 1, 2),
            scratch=56,
        )

    def weight_parts(begun):
        return kernel_call(
            weight_grad_kernel,
            [((width, piece), F32), ((piece, width), F32)],
            16 * rows_here * width * chips * piece,
            weights[0],
            down_own,
            after(kept, begun),
            row_parts[1],
            row_parts[0],
            *others,
            fetch=range(5 + len(others)),
            scratch=56,
        )

    leads, trails, (grad_up, grad_down), (token_grad,) = scatter_blocks(
        keep, send, weight_parts, token_parts
    )
    grad_in, sum_out, grad_router, grad_first_gain, grad_second_gain, table_total = kernel_call(
        functools.partial(finish_kernel, experts, len(leads)),
        [
            ((share, 3 * width), F32),
            ((share, width), F32),
            ((experts, share), F32),
            ((1, share), F32),
            ((1, share), F32),
            ((HEADS, BUCKETS), F32),
        ],
        share * width * 8,
        project_in,
        first_gain[None],
        *leads,
        *trails,
    )
    return (
        mixed,
        token_grad,
        grad_in,
        sum_out,
        grad_router.T,
        grad_first_gain[0],
        grad_second_gain[0],
        table_total.T,
        grad_up[None],
        grad_down[None],
    )


def solution(mesh):
    rows = P(("fsdp", "expert"), None)
    line = P(("fsdp", "expert"))
    up, down = P("expert", None, "fsdp"), P("expert", "fsdp", None)
    return jax.shard_map(
        on_device,
        mesh=mesh,
        in_specs=(rows, rows, rows, rows, rows, line, line, P(), up, down, line, P(), rows, rows),
        out_specs=(rows, rows, rows, rows, rows, line, line, P(), up, down),
        check_vma=False,
    )
```

```python
import functools
import math

import jax
import jax.numpy as jnp
import numpy as np
from jax import lax
from jax.experimental import pallas as pl
from jax.experimental.pallas import tpu as pltpu
from jax.sharding import PartitionSpec as P

HEADS = 12
HEAD = 64
BUCKETS = 32
LANES = 128
BF = jnp.bfloat16
F32 = jnp.float32


def rms_scale(value, gain):
    return value * lax.rsqrt(jnp.mean(value * value, axis=-1, keepdims=True) + 1e-06) * gain


def contract_rows(left, right):
    return lax.dot_general(left, right, (((0,), (0,)), ((), ())), preferred_element_type=F32)


def contract_cols(left, right):
    return lax.dot_general(left, right, (((1,), (1,)), ((), ())), preferred_element_type=F32)


def matmul(left, right):
    return jnp.dot(left, right, preferred_element_type=F32)


AXES = ("fsdp", "expert")


def sizes():
    return lax.axis_size("fsdp"), lax.axis_size("expert")


def core_mask():
    return sizes()[1]


def xy_masks():
    columns, experts = sizes()
    return [2 * experts * x + y for y in range(2) for x in range(columns // 2)]


def chip_masks():
    columns, experts = sizes()
    return [2 * experts * x for x in range(columns // 2)]


def z_bits():
    experts = sizes()[1]
    return [1 << bit for bit in range(1, experts.bit_length() - 1)]


def chip_bits():
    columns, experts = sizes()
    return [experts << bit for bit in range(1, columns.bit_length() - 1)]


def z_masks():
    order = [0]
    for mask in reversed(z_bits()):
        order = order + [k + mask for k in order]
    return order


def block_masks():
    return [c + xy + z for c in (0, core_mask()) for xy in xy_masks() for z in z_masks()]


def swap(value, mask):
    columns, experts = sizes()
    return lax.ppermute(value, AXES, [(i, i ^ mask) for i in range(columns * experts)])


def tied(value, other):
    return lax.optimization_barrier((value, other))[0]


def fan(value, masks):
    return [value] + [swap(value, mask) for mask in masks[1:]]


def stack(parts):
    return jnp.concatenate(parts, axis=0)


def after(value, *others):
    return pl.pallas_call(
        lambda *refs: None,
        out_shape=jax.ShapeDtypeStruct(value.shape, value.dtype),
        in_specs=[pl.BlockSpec(memory_space=pl.ANY)] * (1 + len(others)),
        out_specs=pl.BlockSpec(memory_space=pl.ANY),
        input_output_aliases={0: 0},
    )(value, *others)


def gather_blocks(value, early, late):
    value = stack(fan(value, z_masks()))
    value = after(stack(fan(after(value, *early), xy_masks())), *late)
    return value, swap(value, core_mask())


def add_low(own, arrived):
    return (own.astype(F32) + arrived.astype(F32)).astype(BF)


def sum_of(refs):
    return sum((ref[...].astype(F32) for ref in refs[1:]), refs[0][...].astype(F32))


def sum_kernel(inputs, *refs):
    total = sum_of(refs[:inputs])
    rows = total.shape[0] // (len(refs) - inputs)
    for i, ref in enumerate(refs[inputs:]):
        ref[...] = total[i * rows : (i + 1) * rows].astype(BF)


def sum_apart(parts, pieces):
    rows, width = parts[0].shape
    outs = [((rows // pieces, width), BF)] * pieces
    return kernel_call(functools.partial(sum_kernel, len(parts)), outs, rows * width, *parts)


def halves_of(total, rows):
    runs = [total[at : at + rows].astype(BF) for at in range(0, total.shape[0], rows)]
    return jnp.concatenate(runs[::2], axis=0), jnp.concatenate(runs[1::2], axis=0)


def halve_kernel(rows, own, arrived, keep_ref, send_ref):
    keep_ref[...], send_ref[...] = halves_of(sum_of((own, arrived)), rows)


def halve(own, arrived, rows, near):
    outs = [((own.shape[0] // 2, own.shape[1]), BF)] * 2
    body = functools.partial(halve_kernel, rows)
    return kernel_call(body, outs, own.size, own, arrived, near=near)


def begin_kernel(cut, rows, own, arrived, *refs):
    total = sum_of((own, arrived))
    *leads, keep_ref, send_ref = refs
    count = total.shape[0] // len(leads)
    for i, ref in enumerate(leads):
        ref[...] = total[i * count : (i + 1) * count, :cut].astype(BF)
    keep_ref[...], send_ref[...] = halves_of(total[:, cut:], rows)


def scatter_blocks(value, other, first, second):
    xy, z = xy_masks(), z_masks()
    count, width = value.shape
    share = count // (len(xy) * len(z))
    cut = 3 * (width // LANES) // 4 * LANES
    bits = z_bits()
    steps = [(mask, share << (len(bits) - 1 - i)) for i, mask in enumerate(bits)]
    bits = [1, *reversed(chip_bits())]
    steps += [(mask, share << (len(bits) - 1 - i)) for i, mask in enumerate(bits)]
    *leads, keep, send = kernel_call(
        functools.partial(begin_kernel, cut, steps[0][1]),
        [((count // len(xy), cut), BF)] * len(xy) + [((count // 2, width - cut), BF)] * 2,
        value.size,
        value,
        swap(other, core_mask()),
    )
    arrived = fan_sends(leads, xy)
    done = first(leads[0])
    for i, (mask, _) in enumerate(steps):
        come = swap(send, mask)
        if i + 1 == len(steps):
            break
        near = list(sums[:1]) if i == len(z_bits()) else []
        near += list(done[-1:]) if i == 1 else []
        keep, send = halve(keep, come, steps[i + 1][1], near)
        if i == 0:
            sums = sum_apart([leads[0], *arrived], len(z))
    later = second(sums[0])
    return [sums[0], *fan_sends(sums, z)], [keep, come], done, later


def fan_sends(parts, masks):
    return [swap(part, mask) for part, mask in zip(parts[1:], masks[1:])]


def exchange(value):
    experts = lax.axis_size("expert")
    blocks = value.reshape(experts, value.shape[0] // experts, value.shape[1])
    moved = lax.all_to_all(blocks, "expert", split_axis=0, concat_axis=0, tiled=True)
    return moved.reshape(value.shape)


def lanes_of(value, place):
    high = value.astype(BF)
    rest = (value - high.astype(F32)).astype(BF)
    lane = lax.broadcasted_iota(jnp.int32, (value.shape[0], LANES), 1)
    nothing = jnp.zeros((), BF)
    return jnp.where(lane == place, high, jnp.where(lane == place + 1, rest, nothing))


def nt(left, right):
    return contract_cols(left, right)


def tn(left, right):
    return contract_rows(left, right)


class Incoming:
    def __init__(self, ref, copy):
        self.ref, self.copy = ref, copy
        self.shape, self.dtype = ref.shape, ref.dtype
        copy.start()

    def wait(self):
        if self.copy is not None:
            self.copy.wait()
            self.copy = None

    def __getitem__(self, index):
        self.wait()
        return self.ref[index]


def kernel_call(body, outs, flops, *operands, fetch=(), push=(), near=(), scratch=16):
    moved = sum(math.prod(v.shape) * v.dtype.itemsize for v in operands)
    moved += sum(math.prod(shape) * jnp.dtype(kind).itemsize for shape, kind in outs)
    taken = len(operands)
    fetch = [
        item if isinstance(item, tuple) else (item, ..., operands[item].shape) for item in fetch
    ]
    push = list(push)

    beside = len(near)

    def kernel(*refs):
        refs = refs[:taken] + refs[taken + beside :]
        buffers, refs = refs[taken + len(outs) :], list(refs[: taken + len(outs)])
        arriving, leaving, sent = [], {}, []
        for i, (number, index, _) in enumerate(fetch):
            source = refs[number] if index is ... else refs[number].at[index]
            copy = pltpu.make_async_copy(source, buffers[i], buffers[-1].at[i])
            refs[number] = Incoming(buffers[i], copy)
            arriving.append(refs[number])
        for i, number in enumerate(push, len(fetch)):
            leaving[number] = pltpu.make_async_copy(
                buffers[i], refs[taken + number], buffers[-1].at[i]
            )
            refs[taken + number] = buffers[i]

        def send(number):
            leaving[number].start()
            sent.append(number)

        body(*refs, *([send] if push else []))
        for number in push:
            if number not in sent:
                send(number)
        for value in arriving:
            value.wait()
        for number in push:
            leaving[number].wait()

    whole, left = pl.BlockSpec(memory_space=pltpu.VMEM), pl.BlockSpec(memory_space=pl.ANY)
    fetched = [number for number, _, _ in fetch]
    buffers = [pltpu.VMEM(shape, operands[number].dtype) for number, _, shape in fetch]
    buffers += [pltpu.VMEM(*outs[number]) for number in push]
    if buffers:
        buffers.append(pltpu.SemaphoreType.DMA((len(buffers),)))
    return pl.pallas_call(
        kernel,
        out_shape=[jax.ShapeDtypeStruct(shape, kind) for shape, kind in outs],
        in_specs=[left if i in fetched else whole for i in range(taken)]
        + [whole] * len(near),
        out_specs=[left if i in push else whole for i in range(len(outs))],
        scratch_shapes=buffers,
        compiler_params=pltpu.CompilerParams(vmem_limit_bytes=scratch * 1024 * 1024),
        cost_estimate=pl.CostEstimate(flops=0, bytes_accessed=0, transcendentals=0),
    )(*operands, *near)


def pick_heads(first_head, second_head):
    lane = lax.broadcasted_iota(jnp.int32, first_head.shape, 1)
    return jnp.where(lane < HEAD, first_head, second_head)


def one_head(pair, side):
    lane = lax.broadcasted_iota(jnp.int32, pair.shape, 1)
    return jnp.where((lane < HEAD) == (side == 0), pair, jnp.zeros((), pair.dtype))


def pair_of(value, number):
    return value[:, number * LANES : (number + 1) * LANES]


def inverse_rms(value):
    return lax.rsqrt(jnp.mean(value * value, axis=-1, keepdims=True) + 1e-06)


def small_lanes(experts):
    return -(-(experts + 2) // LANES) * LANES


def shuffle_of(place_of):
    width = place_of.shape[1]
    return (lax.broadcasted_iota(jnp.int32, (width, width), 0) == place_of[...]).astype(BF)


def small_of(lanes, near, far, shuffle):
    end = near.shape[1] - shuffle.shape[0]
    start = end - lanes
    rows = jnp.concatenate([near[:, start:end], far[:, start:end]], axis=0)
    return jnp.transpose(matmul(shuffle, rows)).astype(BF)


def pack_kernel(
    router_rows, first_gain, second_gain, project_in, project_out, down, packed_ref, down_ref
):
    share, columns = project_in.shape
    experts = router_rows.shape[0]
    lanes = packed_ref.shape[1] - columns - project_out.shape[1]
    eye = lax.broadcasted_iota(jnp.int32, (share, share), 0)
    eye = (eye == lax.broadcasted_iota(jnp.int32, (share, share), 1)).astype(BF)
    rows = jnp.concatenate(
        [router_rows[...], first_gain[...], second_gain[...], jnp.zeros((lanes - experts - 2, share), BF)],
        axis=0,
    )
    packed_ref[:, :columns] = project_in[...]
    packed_ref[:, columns : columns + lanes] = nt(eye, rows).astype(BF)
    packed_ref[:, columns + lanes :] = project_out[...]
    down_ref[...] = down[...]


def forward_kernel(
    experts,
    tokens,
    place_of,
    near,
    far,
    bias_rows,
    positions,
    routes,
    target_rows,
    low_ref,
    high_ref,
    outgoing_ref,
    send,
):
    count, width = tokens.shape
    at_probs = width + LANES
    shuffle = shuffle_of(place_of)
    small = small_of(small_lanes(experts), near, far, shuffle)
    half = width // 2
    inputs = tokens[...].astype(F32)
    gain_first = small[experts : experts + 1].astype(F32)
    gain_second = small[experts + 1 : experts + 2].astype(F32)
    normed = (inputs * inverse_rms(inputs) * gain_first).astype(BF)
    normed = matmul(normed, shuffle).astype(BF)
    low_ref[:, 3 * width : 4 * width] = normed
    joint = matmul(normed[:, :half], near[:, : 3 * width])
    joint = joint + matmul(normed[:, half:], far[:, : 3 * width])
    low_ref[:, : 3 * width] = joint.astype(BF)
    row = lax.broadcasted_iota(jnp.int32, (count, count), 0)
    distance = row - lax.broadcasted_iota(jnp.int32, (count, count), 1)
    valid = (distance >= 0) & (distance <= positions[...])
    pairs = width // LANES
    attended = []
    for number in range(pairs):
        query, keys, values = (
            low_ref[:, i * width + number * LANES : i * width + (number + 1) * LANES] for i in range(3)
        )
        outs = []
        for side in range(2):
            head = 2 * number + side
            bias = jnp.broadcast_to(bias_rows[head : head + 1], (count, count))
            bias = pltpu.roll(bias, 0, 1, stride=1, stride_axis=0)
            scores = jnp.where(valid, nt(one_head(query, side), keys) * 0.125 + bias, -1e30)
            expo = jnp.exp(scores - jnp.max(scores, axis=-1, keepdims=True))
            probs = expo / jnp.sum(expo, axis=-1, keepdims=True)
            high_ref[:, at_probs + head * count : at_probs + (head + 1) * count] = probs
            outs.append(matmul(probs.astype(BF), values))
        attended.append(pick_heads(*outs).astype(BF))
    attended = matmul(jnp.concatenate(attended, axis=1), shuffle).astype(BF)
    low_ref[:, 4 * width : 5 * width] = attended
    at = near.shape[1] - width
    first = inputs + matmul(attended[:, :half], near[:, at:])
    first = first + matmul(attended[:, half:], far[:, at:])
    high_ref[:, :width] = first
    second = (first * inverse_rms(first) * gain_second).astype(BF)
    low_ref[:, 5 * width :] = second
    send(0)
    logits = nt(second, small[:LANES])
    lane = lax.broadcasted_iota(jnp.int32, logits.shape, 1)
    chosen = [
        jnp.sum(jnp.where(lane == routes[:, c : c + 1], logits, 0.0), axis=-1, keepdims=True)
        for c in range(2)
    ]
    top = jnp.maximum(chosen[0], chosen[1])
    expo = [jnp.exp(value - top) for value in chosen]
    gates = [value / (expo[0] + expo[1]) for value in expo]
    high_ref[:, width:at_probs] = jnp.where(lane == 0, gates[0], jnp.where(lane == 1, gates[1], 0.0))
    send(1)
    slot = lax.broadcasted_iota(jnp.int32, (outgoing_ref.shape[0], count), 0)
    rows = jnp.zeros(outgoing_ref.shape, F32)
    for c in range(2):
        hot = (slot == target_rows[c : c + 1]).astype(BF)
        rows = rows + matmul(hot, jnp.concatenate([second, lanes_of(gates[c], 0)], axis=1))
    outgoing_ref[...] = rows.astype(BF)


def expert_forward(rows, up):
    inner = nt(rows, up)
    square = inner * inner
    bend = jnp.tanh(0.7978845608028654 * inner * (1.0 + 0.044715 * square))
    slope = 0.5 * (1.0 + bend) + 0.5 * inner * (1.0 - bend * bend) * (
        0.7978845608028654 * (1.0 + 0.134145 * square)
    )
    return (0.5 * inner * (1.0 + bend)).astype(BF), slope


def gate_of(packed, width):
    return packed[:, width : width + 1].astype(F32) + packed[:, width + 1 : width + 2].astype(F32)


def expert_kernel(chips, *refs):
    rows, grads, refs = refs[:2], refs[2:4], refs[4:]
    weights, downs, refs = refs[:chips], refs[chips : 2 * chips], refs[2 * chips :]
    row_refs, kept_ref, shown_ref = refs[:2], refs[2], refs[3]
    count, width = grads[0].shape
    hidden = (weights[0].shape[0] + downs[0].shape[0]) // 2
    late = hidden - downs[0].shape[0]
    for core in range(2):
        packed, grad = rows[core], grads[core][...]
        gate = gate_of(packed, width)
        block = slice(core * count, (core + 1) * count)
        result, row_grad = jnp.zeros((count, width), F32), jnp.zeros((count, width), F32)
        for i in range(chips):
            up, down = weights[i][:hidden], (weights[i][hidden:], downs[i][...])
            active, slope = expert_forward(packed[:, :width], up)
            inner_grad = jnp.concatenate([nt(grad, part) for part in down], axis=1) * slope
            if i == 0:
                kept_ref[block, :hidden] = active
                kept_ref[block, hidden : 2 * hidden] = (inner_grad * gate).astype(BF)
            result = result + matmul(active[:, :late], down[0]) + matmul(active[:, late:], down[1])
            row_grad = row_grad + matmul(inner_grad.astype(BF), up)
        grad = grad.astype(F32)
        scaled = (grad * gate).astype(BF)
        kept_ref[block, 2 * hidden :] = scaled
        row_refs[core][:, :width] = row_grad.astype(BF)
        row_refs[core][:, width:] = result.astype(BF)
    shown_ref[:count] = packed[:, :width]
    shown_ref[count:] = scaled


def weight_grad_kernel(weights, down_late, kept, far, near, *refs):
    others, (up_ref, down_ref, mark_ref) = refs[:-3], refs[-3:]
    mark_ref[...] = jnp.zeros(mark_ref.shape, F32)
    width, hidden = up_ref.shape
    count = near.shape[0]
    up, down = weights[:hidden], (weights[hidden:], down_late[...])
    rows = stack([far[:, :width], near[:, :width]])
    up_grad = tn(rows, kept[:, hidden : 2 * hidden])
    down_grad = tn(kept[:, :hidden], kept[:, 2 * hidden :])
    for pair in zip(others[::2], others[1::2]):
        rows = stack([part[:count] for part in pair])
        scaled = stack([part[count:] for part in pair])
        active, slope = expert_forward(rows, up)
        inner_grad = jnp.concatenate([nt(scaled, part) for part in down], axis=1)
        up_grad = up_grad + tn(rows, (inner_grad * slope).astype(BF))
        down_grad = down_grad + tn(active, scaled)
    up_ref[...] = up_grad
    down_ref[...] = down_grad


def table_lanes(share):
    return BUCKETS * HEADS // share


def home_kernel(
    experts,
    share,
    home,
    routes,
    target,
    cotangent,
    place_of,
    low,
    high,
    near,
    far,
    flip_hot,
    keep_ref,
    send_ref,
    first_grad_ref,
    joint_grad_ref,
    distance_ref,
    mixed_ref,
):
    count, width = cotangent.shape
    half = width // 2
    shuffle = shuffle_of(place_of)
    small_rows = small_of(small_lanes(experts), near, far, shuffle)
    at_probs = width + LANES
    slot = lax.broadcasted_iota(jnp.int32, (count, home.shape[0]), 1)
    lane = lax.broadcasted_iota(jnp.int32, (count, LANES), 1)
    gates = [high[:, width + c : width + c + 1] for c in range(2)]
    routed = [matmul((slot == target[:, c : c + 1]).astype(BF), home[...]) for c in range(2)]
    returned = [value[:, width:] for value in routed]
    upstream = cotangent[...].astype(F32)
    dots = [jnp.sum(upstream * value, axis=-1, keepdims=True) for value in returned]
    mean = gates[0] * dots[0] + gates[1] * dots[1]
    logit_grad = jnp.zeros((count, LANES), F32)
    for c in range(2):
        logit_grad = jnp.where(lane == routes[:, c : c + 1], gates[c] * (dots[c] - mean), logit_grad)
    logit_grad = logit_grad.astype(BF)
    second_grad = gates[0] * routed[0][:, :width] + gates[1] * routed[1][:, :width]
    second_grad = second_grad + matmul(logit_grad, small_rows[:LANES])
    gain = small_rows[experts + 1 : experts + 2].astype(F32)
    first = high[:, :width]
    mixed_ref[...] = (first + gates[0] * returned[0] + gates[1] * returned[1]).astype(BF)
    inverse = inverse_rms(first)
    unit = first * inverse
    scaled = second_grad * gain
    first_grad = upstream + inverse * (
        scaled - unit * jnp.mean(unit * scaled, axis=-1, keepdims=True)
    )
    first_grad_ref[...] = first_grad
    first_low = first_grad.astype(BF)
    attended_grad = jnp.concatenate(
        [nt(first_low, part[:, part.shape[1] - width :]) for part in (near, far)], axis=1
    ).astype(BF)
    attended_grad = nt(attended_grad, shuffle).astype(BF)
    value_grad = []
    for number in range(width // LANES):
        outs = [
            tn(
                high[:, at_probs + head * count : at_probs + (head + 1) * count].astype(BF),
                pair_of(attended_grad, number),
            )
            for head in (2 * number, 2 * number + 1)
        ]
        value_grad.append(pick_heads(*outs).astype(BF))
    value_grad = jnp.concatenate(value_grad, axis=1)
    joint_grad_ref[:, 2 * width :] = value_grad
    gain_part = second_grad * unit
    gain_high = gain_part.astype(BF)
    gain_rest = (gain_part - gain_high.astype(F32)).astype(BF)
    ones = (lane == experts).astype(BF)
    left = jnp.concatenate([low[:, 5 * width :], gain_high, gain_rest], axis=0)
    left = matmul(left, shuffle).astype(BF)
    right = jnp.concatenate([logit_grad, ones, ones], axis=0)
    small = tn(left, right)
    row = lax.broadcasted_iota(jnp.int32, (count, count), 0)
    for number in range(width // LANES):
        span = slice(number * LANES, (number + 1) * LANES)
        query, keys, values = (
            low[:, i * width + number * LANES : i * width + (number + 1) * LANES] for i in range(3)
        )
        own_grad = attended_grad[:, span]
        query_grads, key_grads = [], []
        for side in range(2):
            head = 2 * number + side
            chance = high[:, at_probs + head * count : at_probs + (head + 1) * count]
            prob_grad = nt(one_head(own_grad, side), values)
            score_grad = chance * (prob_grad - jnp.sum(chance * prob_grad, axis=-1, keepdims=True))
            lined = score_grad
            step = 1
            while step < count:
                lined = jnp.where((row // step) % 2 == 1, pltpu.roll(lined, count - step, 1), lined)
                step *= 2
            distance_ref[head : head + 1] = jnp.sum(lined, axis=0, keepdims=True)
            pair_grad = (score_grad * 0.125).astype(BF)
            query_grads.append(matmul(pair_grad, keys))
            key_grads.append(tn(pair_grad, query))
        joint_grad_ref[:, span] = pick_heads(*query_grads).astype(BF)
        joint_grad_ref[:, width + number * LANES : width + (number + 1) * LANES] = pick_heads(
            *key_grads
        ).astype(BF)
    table = jnp.dot(
        distance_ref[...], flip_hot[...], precision=lax.Precision.HIGHEST, preferred_element_type=F32
    ).astype(BF)
    lanes = table_lanes(share)
    spread = keep_ref.shape[1] - 4 * width
    value_row = lax.broadcasted_iota(jnp.int32, (width, HEADS), 0) % share * lanes
    value_head = lax.broadcasted_iota(jnp.int32, (width, HEADS), 1)
    bucket = lax.broadcasted_iota(jnp.int32, (BUCKETS, spread), 0)
    lane = lax.broadcasted_iota(jnp.int32, (BUCKETS, spread), 1) - (experts + 1)
    small = jnp.pad(small, ((0, 0), (0, spread - LANES)))
    for start in range(0, max(lanes, BUCKETS), min(lanes, BUCKETS)):
        if lanes <= BUCKETS:
            picked = (value_row == value_head * BUCKETS + start).astype(BF)
            put = ((lane >= 0) & (lane < lanes) & (bucket == lane + start)).astype(BF)
        else:
            picked = (value_row + start == value_head * BUCKETS).astype(BF)
            put = (lane - start == bucket).astype(BF)
        small = small + matmul(picked, matmul(table, put).astype(BF))
    joint_grads = joint_grad_ref[...]
    for ref, at in ((keep_ref, 0), (send_ref, half)):
        attended, normed = (low[:, i * width + at : i * width + at + half] for i in (4, 3))
        ref[:, : 3 * width] = tn(normed, joint_grads).astype(BF)
        ref[:, 3 * width : 4 * width] = tn(attended, first_low).astype(BF)
        ref[:, 4 * width :] = small[at : at + half].astype(BF)


def token_kernel(
    experts,
    tokens,
    first_grad,
    joint_grad,
    near,
    far,
    place_of,
    token_ref,
    mark_ref,
):
    width = tokens.shape[1]
    shuffle = shuffle_of(place_of)
    gain = small_of(small_lanes(experts), near, far, shuffle)[experts : experts + 1].astype(F32)
    grads = joint_grad[...]
    normed_grad = jnp.concatenate(
        [nt(grads, part[:, : 3 * width]) for part in (near, far)], axis=1
    )
    large = normed_grad.astype(BF)
    rest = (normed_grad - large.astype(F32)).astype(BF)
    scaled = (nt(large, shuffle) + nt(rest, shuffle)) * gain
    inputs = tokens[...].astype(F32)
    inverse = inverse_rms(inputs)
    unit = inputs * inverse
    input_grad = inverse * (scaled - unit * jnp.mean(unit * scaled, axis=-1, keepdims=True))
    mark_ref[...] = jnp.zeros(mark_ref.shape, F32)
    token_ref[...] = (first_grad[...] + input_grad).astype(BF)


def finish_kernel(experts, leads, project_in, gain, *refs):
    parts, refs = refs[:-6], refs[-6:]
    grad_in_ref, sum_out_ref, router_ref, first_gain_ref, second_gain_ref, table_ref = refs
    sums = jnp.concatenate([sum_of(parts[:leads]), sum_of(parts[leads:])], axis=1)
    share, width = sum_out_ref.shape
    grad_in = sums[:, : 3 * width]
    grad_in_ref[...] = grad_in
    sum_out_ref[...] = sums[:, 3 * width : 4 * width]
    small = sums[:, 4 * width :]
    row = lax.broadcasted_iota(jnp.int32, (share, share), 0)
    same = row == lax.broadcasted_iota(jnp.int32, (share, share), 1)

    router_ref[...] = lax.dot_general(
        small[:, :experts],
        same.astype(F32),
        (((0,), (0,)), ((), ())),
        precision=lax.Precision.HIGHEST,
        preferred_element_type=F32,
    )

    def lined(column):
        return jnp.sum(jnp.where(same, column, 0.0), axis=0, keepdims=True)

    second_gain_ref[...] = lined(small[:, experts : experts + 1])
    grads = jnp.sum(grad_in * project_in[...].astype(F32), axis=-1, keepdims=True)
    first_gain_ref[...] = lined(grads) / gain[...].astype(F32)
    lanes = table_lanes(share)
    table = small[:, experts + 1 : experts + 1 + lanes]
    value_row = lax.broadcasted_iota(jnp.int32, (share, HEADS), 0) * lanes
    value_head = lax.broadcasted_iota(jnp.int32, (share, HEADS), 1)
    step = min(lanes, BUCKETS)
    total = jnp.zeros((HEADS, BUCKETS), F32)
    for start in range(0, max(lanes, BUCKETS), step):
        if lanes <= BUCKETS:
            picked, part = value_row == value_head * BUCKETS + start, table
        else:
            picked = value_row + start == value_head * BUCKETS
            part = table[:, start : start + step]
        put = lax.dot_general(
            picked.astype(F32),
            part,
            (((0,), (0,)), ((), ())),
            precision=lax.Precision.HIGHEST,
            preferred_element_type=F32,
        )
        if lanes <= BUCKETS:
            table_ref[:, start : start + step] = put
        else:
            total = total + put
            table_ref[...] = total


def on_device(
    tokens,
    cotangent,
    project_in,
    project_out,
    router,
    first_gain,
    second_gain,
    bias_table,
    expert_up,
    expert_down,
    positions,
    buckets,
    routes,
    slots,
):
    highest = lax.Precision.HIGHEST
    count, width = tokens.shape
    experts = lax.axis_size("expert")
    capacity = 3 * count // experts
    rows_here = experts * capacity
    share = project_in.shape[0]
    column = lax.axis_index("fsdp")
    mine = column * experts + lax.axis_index("expert")
    target = routes * capacity + slots
    slot_index = jnp.arange(rows_here, dtype=jnp.int32)
    hot = (slot_index[None, None, :] == jnp.transpose(target)[:, :, None]).astype(BF)
    place_hot = hot[0] + hot[1]
    grad_rows = contract_rows(place_hot, cotangent).astype(BF)
    grad_own = exchange(grad_rows)

    lanes = small_lanes(experts)
    hidden = expert_down.shape[1]
    late = hidden - hidden // 3
    packed, down_own = kernel_call(
        pack_kernel,
        [((share, lanes + 4 * width), BF), ((hidden - late, width), BF)],
        0,
        router.T,
        first_gain[None],
        second_gain[None],
        project_in,
        project_out,
        expert_down,
        fetch=(*range(5), (5, (0, slice(late, hidden)), (hidden - late, width))),
        scratch=56,
    )
    weights = stack([expert_up[0].T, expert_down[0, :late]])
    downs = fan(down_own, chip_masks())
    halves = gather_blocks(packed, (weights, *downs[1:]), (grad_own,))
    grad_parts = (grad_own, swap(grad_own, core_mask()))
    weights = fan(after(weights, halves[0]), chip_masks())
    feature = jnp.arange(width, dtype=jnp.int32)
    masks = jnp.asarray(np.repeat(np.array(block_masks(), np.int32), share))
    place_of = (masks ^ mine) * share + feature % share


    places = jnp.arange(count, dtype=jnp.int32)
    bucket_hot = (buckets[:, None] == jnp.arange(BUCKETS, dtype=jnp.int32)).astype(F32)
    flip = ((places[:, None] + places[None, :]) % count == 0).astype(F32)
    flip_hot = jnp.dot(flip, bucket_hot, precision=highest)
    bias_rows = lax.dot_general(
        bias_table, flip_hot, (((0,), (1,)), ((), ())), precision=highest
    )
    low, high, outgoing = kernel_call(
        functools.partial(forward_kernel, experts),
        [
            ((count, 6 * width), BF),
            ((count, width + LANES + HEADS * count), F32),
            ((rows_here, width + LANES), BF),
        ],
        2 * count * width * 6 * width,
        tokens,
        place_of[None],
        *halves,
        bias_rows,
        positions[:, None],
        routes,
        jnp.transpose(target),
        fetch=(0, 2, 3, 1, 4, 5, 6, 7),
        push=(0, 1, 2),
        scratch=56,
    )
    row_own = exchange(outgoing)
    row_parts = (row_own, swap(row_own, core_mask()))

    chips = len(chip_masks())
    piece = expert_up.shape[2]
    wide = (rows_here, 2 * width)
    row_far, row_near, kept, shown = kernel_call(
        functools.partial(expert_kernel, chips),
        [
            (wide, BF),
            (wide, BF),
            ((2 * rows_here, 2 * piece + width), BF),
            ((2 * rows_here, width), BF),
        ],
        16 * rows_here * width * chips * piece,
        row_parts[1],
        row_parts[0],
        grad_parts[1],
        grad_parts[0],
        *weights,
        *downs,
        fetch=range(4, 4 + 2 * chips),
        scratch=50,
    )
    others = [swap(shown, mask) for mask in chip_masks()[1:]]
    others = [both for part in others for both in (part, swap(part, core_mask()))]
    (row_sum,) = sum_apart([row_near, swap(row_far, core_mask())], 1)
    home = after(exchange(row_sum), *others)

    half = width // 2
    table_at = experts + 1
    spread_lanes = -(-(table_at + table_lanes(share)) // LANES) * LANES
    keep, send, first_grad, joint_grad, _, mixed = kernel_call(
        functools.partial(home_kernel, experts, share),
        [
            ((half, 4 * width + spread_lanes), BF),
            ((half, 4 * width + spread_lanes), BF),
            ((count, width), F32),
            ((count, 3 * width), BF),
            ((HEADS, count), F32),
            ((count, width), BF),
        ],
        2 * count * width * 10 * width,
        home,
        routes,
        target,
        cotangent,
        place_of[None],
        low,
        high,
        *halves,
        flip_hot,
        fetch=(
            6,
            (7, (slice(None), slice(3 * width, None)), (half, lanes + width)),
            (8, (slice(None), slice(3 * width, None)), (half, lanes + width)),
            3,
            5,
        ),
        scratch=50,
    )
    def token_parts(begun):
        return kernel_call(
            functools.partial(token_kernel, experts),
            [((count, width), BF), ((8, LANES), F32)],
            2 * count * width * 6 * width,
            tokens,
            first_grad,
            joint_grad,
            *halves,
            place_of[None],
            fetch=(3, 4, 0, 1, 2),
            near=(begun,),
            scratch=56,
        )

    def weight_parts(begun):
        return kernel_call(
            weight_grad_kernel,
            [((width, piece), F32), ((piece, width), F32), ((8, LANES), F32)],
            16 * rows_here * width * chips * piece,
            weights[0],
            down_own,
            kept,
            row_parts[1],
            row_parts[0],
            *others,
            fetch=range(5 + len(others)),
            near=(begun,),
            scratch=56,
        )

    leads, trails, (grad_up, grad_down, _), (token_grad, mark) = scatter_blocks(
        keep, send, weight_parts, token_parts
    )
    grad_in, sum_out, grad_router, grad_first_gain, grad_second_gain, table_total = kernel_call(
        functools.partial(finish_kernel, experts, len(leads)),
        [
            ((share, 3 * width), F32),
            ((share, width), F32),
            ((experts, share), F32),
            ((1, share), F32),
            ((1, share), F32),
            ((HEADS, BUCKETS), F32),
        ],
        share * width * 8,
        project_in,
        first_gain[None],
        *leads,
        *trails,
        near=(mark,),
    )
    return (
        mixed,
        token_grad,
        grad_in,
        sum_out,
        grad_router.T,
        grad_first_gain[0],
        grad_second_gain[0],
        table_total.T,
        grad_up[None],
        grad_down[None],
    )


def solution(mesh):
    rows = P(("fsdp", "expert"), None)
    line = P(("fsdp", "expert"))
    up, down = P("expert", None, "fsdp"), P("expert", "fsdp", None)
    return jax.shard_map(
        on_device,
        mesh=mesh,
        in_specs=(rows, rows, rows, rows, rows, line, line, P(), up, down, line, P(), rows, rows),
        out_specs=(rows, rows, rows, rows, rows, line, line, P(), up, down),
        check_vma=False,
    )
```

```python
import functools
import math

import jax
import jax.numpy as jnp
import numpy as np
from jax import lax
from jax.experimental import pallas as pl
from jax.experimental.pallas import tpu as pltpu
from jax.sharding import PartitionSpec as P

HEADS = 12
HEAD = 64
BUCKETS = 32
LANES = 128
BF = jnp.bfloat16
F32 = jnp.float32


def rms_scale(value, gain):
    return value * lax.rsqrt(jnp.mean(value * value, axis=-1, keepdims=True) + 1e-06) * gain


def contract_rows(left, right):
    return lax.dot_general(left, right, (((0,), (0,)), ((), ())), preferred_element_type=F32)


def contract_cols(left, right):
    return lax.dot_general(left, right, (((1,), (1,)), ((), ())), preferred_element_type=F32)


def matmul(left, right):
    return jnp.dot(left, right, preferred_element_type=F32)


AXES = ("fsdp", "expert")


def sizes():
    return lax.axis_size("fsdp"), lax.axis_size("expert")


def core_mask():
    return sizes()[1]


def xy_masks():
    columns, experts = sizes()
    return [2 * experts * x + y for y in range(2) for x in range(columns // 2)]


def chip_masks():
    columns, experts = sizes()
    return [2 * experts * x for x in range(columns // 2)]


def z_bits():
    experts = sizes()[1]
    return [1 << bit for bit in range(1, experts.bit_length() - 1)]


def chip_bits():
    columns, experts = sizes()
    return [experts << bit for bit in range(1, columns.bit_length() - 1)]


def z_masks():
    order = [0]
    for mask in reversed(z_bits()):
        order = order + [k + mask for k in order]
    return order


def block_masks():
    return [c + xy + z for c in (0, core_mask()) for xy in xy_masks() for z in z_masks()]


def swap(value, mask):
    columns, experts = sizes()
    return lax.ppermute(value, AXES, [(i, i ^ mask) for i in range(columns * experts)])


def tied(value, other):
    return lax.optimization_barrier((value, other))[0]


def fan(value, masks):
    return [value] + [swap(value, mask) for mask in masks[1:]]


def stack(parts):
    return jnp.concatenate(parts, axis=0)


def after(value, *others):
    return pl.pallas_call(
        lambda *refs: None,
        out_shape=jax.ShapeDtypeStruct(value.shape, value.dtype),
        in_specs=[pl.BlockSpec(memory_space=pl.ANY)] * (1 + len(others)),
        out_specs=pl.BlockSpec(memory_space=pl.ANY),
        input_output_aliases={0: 0},
    )(value, *others)


def gather_blocks(value, early, late):
    value = stack(fan(value, z_masks()))
    value = after(stack(fan(after(value, *early), xy_masks())), *late)
    return value, swap(value, core_mask())


def add_low(own, arrived):
    return (own.astype(F32) + arrived.astype(F32)).astype(BF)


def sum_of(refs):
    return sum((ref[...].astype(F32) for ref in refs[1:]), refs[0][...].astype(F32))


def sum_kernel(inputs, *refs):
    total = sum_of(refs[:inputs])
    rows = total.shape[0] // (len(refs) - inputs)
    for i, ref in enumerate(refs[inputs:]):
        ref[...] = total[i * rows : (i + 1) * rows].astype(BF)


def sum_apart(parts, pieces):
    rows, width = parts[0].shape
    outs = [((rows // pieces, width), BF)] * pieces
    return kernel_call(functools.partial(sum_kernel, len(parts)), outs, rows * width, *parts)


def halves_of(total, rows):
    runs = [total[at : at + rows].astype(BF) for at in range(0, total.shape[0], rows)]
    return jnp.concatenate(runs[::2], axis=0), jnp.concatenate(runs[1::2], axis=0)


def halve_kernel(rows, own, arrived, keep_ref, send_ref):
    keep_ref[...], send_ref[...] = halves_of(sum_of((own, arrived)), rows)


def halve(own, arrived, rows, near):
    outs = [((own.shape[0] // 2, own.shape[1]), BF)] * 2
    body = functools.partial(halve_kernel, rows)
    return kernel_call(body, outs, own.size, own, arrived, near=near)


def begin_kernel(cut, rows, own, arrived, *refs):
    total = sum_of((own, arrived))
    *leads, keep_ref, send_ref = refs
    count = total.shape[0] // len(leads)
    for i, ref in enumerate(leads):
        ref[...] = total[i * count : (i + 1) * count, :cut].astype(BF)
    keep_ref[...], send_ref[...] = halves_of(total[:, cut:], rows)


def scatter_blocks(value, other, first, second):
    xy, z = xy_masks(), z_masks()
    count, width = value.shape
    share = count // (len(xy) * len(z))
    cut = 3 * (width // LANES) // 4 * LANES
    bits = z_bits()
    steps = [(mask, share << (len(bits) - 1 - i)) for i, mask in enumerate(bits)]
    bits = [1, *reversed(chip_bits())]
    steps += [(mask, share << (len(bits) - 1 - i)) for i, mask in enumerate(bits)]
    *leads, keep, send = kernel_call(
        functools.partial(begin_kernel, cut, steps[0][1]),
        [((count // len(xy), cut), BF)] * len(xy) + [((count // 2, width - cut), BF)] * 2,
        value.size,
        value,
        swap(other, core_mask()),
    )
    arrived = fan_sends(leads, xy)
    done = first(leads[0])
    for i, (mask, _) in enumerate(steps):
        come = swap(send, mask)
        if i + 1 == len(steps):
            break
        near = list(sums[:1]) if i == len(z_bits()) else []
        near += list(done[-1:]) if i == 1 else []
        keep, send = halve(keep, come, steps[i + 1][1], near)
        if i == 0:
            sums = sum_apart([leads[0], *arrived], len(z))
    later = second(sums[0])
    return [sums[0], *fan_sends(sums, z)], [keep, come], done, later


def fan_sends(parts, masks):
    return [swap(part, mask) for part, mask in zip(parts[1:], masks[1:])]


def exchange(value):
    experts = lax.axis_size("expert")
    blocks = value.reshape(experts, value.shape[0] // experts, value.shape[1])
    moved = lax.all_to_all(blocks, "expert", split_axis=0, concat_axis=0, tiled=True)
    return moved.reshape(value.shape)


def lanes_of(value, place):
    high = value.astype(BF)
    rest = (value - high.astype(F32)).astype(BF)
    lane = lax.broadcasted_iota(jnp.int32, (value.shape[0], LANES), 1)
    nothing = jnp.zeros((), BF)
    return jnp.where(lane == place, high, jnp.where(lane == place + 1, rest, nothing))


def nt(left, right):
    return contract_cols(left, right)


def tn(left, right):
    return contract_rows(left, right)


class Incoming:
    def __init__(self, ref, copy):
        self.ref, self.copy = ref, copy
        self.shape, self.dtype = ref.shape, ref.dtype
        copy.start()

    def wait(self):
        if self.copy is not None:
            self.copy.wait()
            self.copy = None

    def __getitem__(self, index):
        self.wait()
        return self.ref[index]


def kernel_call(body, outs, flops, *operands, fetch=(), push=(), near=(), scratch=16):
    moved = sum(math.prod(v.shape) * v.dtype.itemsize for v in operands)
    moved += sum(math.prod(shape) * jnp.dtype(kind).itemsize for shape, kind in outs)
    taken = len(operands)
    fetch = [
        item if isinstance(item, tuple) else (item, ..., operands[item].shape) for item in fetch
    ]
    push = list(push)

    beside = len(near)

    def kernel(*refs):
        refs = refs[:taken] + refs[taken + beside :]
        buffers, refs = refs[taken + len(outs) :], list(refs[: taken + len(outs)])
        arriving, leaving, sent = [], {}, []
        for i, (number, index, _) in enumerate(fetch):
            source = refs[number] if index is ... else refs[number].at[index]
            copy = pltpu.make_async_copy(source, buffers[i], buffers[-1].at[i])
            refs[number] = Incoming(buffers[i], copy)
            arriving.append(refs[number])
        for i, number in enumerate(push, len(fetch)):
            leaving[number] = pltpu.make_async_copy(
                buffers[i], refs[taken + number], buffers[-1].at[i]
            )
            refs[taken + number] = buffers[i]

        def send(number):
            leaving[number].start()
            sent.append(number)

        body(*refs, *([send] if push else []))
        for number in push:
            if number not in sent:
                send(number)
        for value in arriving:
            value.wait()
        for number in push:
            leaving[number].wait()

    whole, left = pl.BlockSpec(memory_space=pltpu.VMEM), pl.BlockSpec(memory_space=pl.ANY)
    fetched = [number for number, _, _ in fetch]
    buffers = [pltpu.VMEM(shape, operands[number].dtype) for number, _, shape in fetch]
    buffers += [pltpu.VMEM(*outs[number]) for number in push]
    if buffers:
        buffers.append(pltpu.SemaphoreType.DMA((len(buffers),)))
    return pl.pallas_call(
        kernel,
        out_shape=[jax.ShapeDtypeStruct(shape, kind) for shape, kind in outs],
        in_specs=[left if i in fetched else whole for i in range(taken)]
        + [whole] * len(near),
        out_specs=[left if i in push else whole for i in range(len(outs))],
        scratch_shapes=buffers,
        compiler_params=pltpu.CompilerParams(vmem_limit_bytes=scratch * 1024 * 1024),
        cost_estimate=pl.CostEstimate(flops=0, bytes_accessed=0, transcendentals=0),
    )(*operands, *near)


def pick_heads(first_head, second_head):
    lane = lax.broadcasted_iota(jnp.int32, first_head.shape, 1)
    return jnp.where(lane < HEAD, first_head, second_head)


def one_head(pair, side):
    lane = lax.broadcasted_iota(jnp.int32, pair.shape, 1)
    return jnp.where((lane < HEAD) == (side == 0), pair, jnp.zeros((), pair.dtype))


def pair_of(value, number):
    return value[:, number * LANES : (number + 1) * LANES]


def inverse_rms(value):
    return lax.rsqrt(jnp.mean(value * value, axis=-1, keepdims=True) + 1e-06)


def small_lanes(experts):
    return -(-(experts + 2) // LANES) * LANES


def shuffle_of(place_of):
    width = place_of.shape[1]
    return (lax.broadcasted_iota(jnp.int32, (width, width), 0) == place_of[...]).astype(BF)


def small_of(lanes, near, far, shuffle):
    end = near.shape[1] - shuffle.shape[0]
    start = end - lanes
    rows = jnp.concatenate([near[:, start:end], far[:, start:end]], axis=0)
    return jnp.transpose(matmul(shuffle, rows)).astype(BF)


def pack_kernel(
    router_rows, first_gain, second_gain, project_in, project_out, down, packed_ref, down_ref
):
    share, columns = project_in.shape
    experts = router_rows.shape[0]
    lanes = packed_ref.shape[1] - columns - project_out.shape[1]
    eye = lax.broadcasted_iota(jnp.int32, (share, share), 0)
    eye = (eye == lax.broadcasted_iota(jnp.int32, (share, share), 1)).astype(BF)
    rows = jnp.concatenate(
        [router_rows[...], first_gain[...], second_gain[...], jnp.zeros((lanes - experts - 2, share), BF)],
        axis=0,
    )
    packed_ref[:, :columns] = project_in[...]
    packed_ref[:, columns : columns + lanes] = nt(eye, rows).astype(BF)
    packed_ref[:, columns + lanes :] = project_out[...]
    down_ref[...] = down[...]


def forward_kernel(
    experts,
    tokens,
    place_of,
    near,
    far,
    bias_rows,
    positions,
    routes,
    target_rows,
    low_ref,
    high_ref,
    outgoing_ref,
    send,
):
    count, width = tokens.shape
    at_probs = width + LANES
    shuffle = shuffle_of(place_of)
    small = small_of(small_lanes(experts), near, far, shuffle)
    half = width // 2
    inputs = tokens[...].astype(F32)
    gain_first = small[experts : experts + 1].astype(F32)
    gain_second = small[experts + 1 : experts + 2].astype(F32)
    normed = (inputs * inverse_rms(inputs) * gain_first).astype(BF)
    normed = matmul(normed, shuffle).astype(BF)
    low_ref[:, 3 * width : 4 * width] = normed
    joint = matmul(normed[:, :half], near[:, : 3 * width])
    joint = joint + matmul(normed[:, half:], far[:, : 3 * width])
    low_ref[:, : 3 * width] = joint.astype(BF)
    row = lax.broadcasted_iota(jnp.int32, (count, count), 0)
    distance = row - lax.broadcasted_iota(jnp.int32, (count, count), 1)
    valid = (distance >= 0) & (distance <= positions[...])
    pairs = width // LANES
    attended = []
    for number in range(pairs):
        query, keys, values = (
            low_ref[:, i * width + number * LANES : i * width + (number + 1) * LANES] for i in range(3)
        )
        outs = []
        for side in range(2):
            head = 2 * number + side
            bias = jnp.broadcast_to(bias_rows[head : head + 1], (count, count))
            bias = pltpu.roll(bias, 0, 1, stride=1, stride_axis=0)
            scores = jnp.where(valid, nt(one_head(query, side), keys) * 0.125 + bias, -1e30)
            expo = jnp.exp(scores - jnp.max(scores, axis=-1, keepdims=True))
            probs = expo / jnp.sum(expo, axis=-1, keepdims=True)
            high_ref[:, at_probs + head * count : at_probs + (head + 1) * count] = probs
            outs.append(matmul(probs.astype(BF), values))
        attended.append(pick_heads(*outs).astype(BF))
    attended = matmul(jnp.concatenate(attended, axis=1), shuffle).astype(BF)
    low_ref[:, 4 * width : 5 * width] = attended
    at = near.shape[1] - width
    first = inputs + matmul(attended[:, :half], near[:, at:])
    first = first + matmul(attended[:, half:], far[:, at:])
    high_ref[:, :width] = first
    second = (first * inverse_rms(first) * gain_second).astype(BF)
    low_ref[:, 5 * width :] = second
    send(0)
    logits = nt(second, small[:LANES])
    lane = lax.broadcasted_iota(jnp.int32, logits.shape, 1)
    chosen = [
        jnp.sum(jnp.where(lane == routes[:, c : c + 1], logits, 0.0), axis=-1, keepdims=True)
        for c in range(2)
    ]
    top = jnp.maximum(chosen[0], chosen[1])
    expo = [jnp.exp(value - top) for value in chosen]
    gates = [value / (expo[0] + expo[1]) for value in expo]
    high_ref[:, width:at_probs] = jnp.where(lane == 0, gates[0], jnp.where(lane == 1, gates[1], 0.0))
    send(1)
    slot = lax.broadcasted_iota(jnp.int32, (outgoing_ref.shape[0], count), 0)
    rows = jnp.zeros(outgoing_ref.shape, F32)
    for c in range(2):
        hot = (slot == target_rows[c : c + 1]).astype(BF)
        rows = rows + matmul(hot, jnp.concatenate([second, lanes_of(gates[c], 0)], axis=1))
    outgoing_ref[...] = rows.astype(BF)


def expert_forward(rows, up):
    inner = nt(rows, up)
    square = inner * inner
    bend = jnp.tanh(0.7978845608028654 * inner * (1.0 + 0.044715 * square))
    slope = 0.5 * (1.0 + bend) + 0.5 * inner * (1.0 - bend * bend) * (
        0.7978845608028654 * (1.0 + 0.134145 * square)
    )
    return (0.5 * inner * (1.0 + bend)).astype(BF), slope


def gate_of(packed, width):
    return packed[:, width : width + 1].astype(F32) + packed[:, width + 1 : width + 2].astype(F32)


def expert_kernel(chips, *refs):
    rows, grads, refs = refs[:2], refs[2:4], refs[4:]
    weights, downs, refs = refs[:chips], refs[chips : 2 * chips], refs[2 * chips :]
    row_refs, kept_ref, shown_ref = refs[:2], refs[2], refs[3]
    count, width = grads[0].shape
    hidden = (weights[0].shape[0] + downs[0].shape[0]) // 2
    late = hidden - downs[0].shape[0]
    for core in range(2):
        packed, grad = rows[core], grads[core][...]
        gate = gate_of(packed, width)
        block = slice(core * count, (core + 1) * count)
        result, row_grad = jnp.zeros((count, width), F32), jnp.zeros((count, width), F32)
        for i in range(chips):
            up, down = weights[i][:hidden], (weights[i][hidden:], downs[i][...])
            active, slope = expert_forward(packed[:, :width], up)
            inner_grad = jnp.concatenate([nt(grad, part) for part in down], axis=1) * slope
            if i == 0:
                kept_ref[block, :hidden] = active
                kept_ref[block, hidden : 2 * hidden] = (inner_grad * gate).astype(BF)
            result = result + matmul(active[:, :late], down[0]) + matmul(active[:, late:], down[1])
            row_grad = row_grad + matmul(inner_grad.astype(BF), up)
        grad = grad.astype(F32)
        scaled = (grad * gate).astype(BF)
        kept_ref[block, 2 * hidden :] = scaled
        row_refs[core][:, :width] = row_grad.astype(BF)
        row_refs[core][:, width:] = result.astype(BF)
    shown_ref[:count] = packed[:, :width]
    shown_ref[count:] = scaled


def weight_grad_kernel(weights, down_late, kept, far, near, *refs):
    others, (up_ref, down_ref, mark_ref) = refs[:-3], refs[-3:]
    mark_ref[...] = jnp.zeros(mark_ref.shape, F32)
    width, hidden = up_ref.shape
    count = near.shape[0]
    up, down = weights[:hidden], (weights[hidden:], down_late[...])
    rows = stack([far[:, :width], near[:, :width]])
    up_grad = tn(rows, kept[:, hidden : 2 * hidden])
    down_grad = tn(kept[:, :hidden], kept[:, 2 * hidden :])
    for pair in zip(others[::2], others[1::2]):
        rows = stack([part[:count] for part in pair])
        scaled = stack([part[count:] for part in pair])
        active, slope = expert_forward(rows, up)
        inner_grad = jnp.concatenate([nt(scaled, part) for part in down], axis=1)
        up_grad = up_grad + tn(rows, (inner_grad * slope).astype(BF))
        down_grad = down_grad + tn(active, scaled)
    up_ref[...] = up_grad
    down_ref[...] = down_grad


def table_lanes(share):
    return BUCKETS * HEADS // share


def home_kernel(
    experts,
    share,
    home,
    routes,
    target,
    cotangent,
    place_of,
    low,
    high,
    near,
    far,
    flip_hot,
    keep_ref,
    send_ref,
    first_grad_ref,
    joint_grad_ref,
    distance_ref,
    mixed_ref,
):
    count, width = cotangent.shape
    half = width // 2
    shuffle = shuffle_of(place_of)
    small_rows = small_of(small_lanes(experts), near, far, shuffle)
    at_probs = width + LANES
    slot = lax.broadcasted_iota(jnp.int32, (count, home.shape[0]), 1)
    lane = lax.broadcasted_iota(jnp.int32, (count, LANES), 1)
    gates = [high[:, width + c : width + c + 1] for c in range(2)]
    routed = [matmul((slot == target[:, c : c + 1]).astype(BF), home[...]) for c in range(2)]
    returned = [value[:, width:] for value in routed]
    upstream = cotangent[...].astype(F32)
    dots = [jnp.sum(upstream * value, axis=-1, keepdims=True) for value in returned]
    mean = gates[0] * dots[0] + gates[1] * dots[1]
    logit_grad = jnp.zeros((count, LANES), F32)
    for c in range(2):
        logit_grad = jnp.where(lane == routes[:, c : c + 1], gates[c] * (dots[c] - mean), logit_grad)
    logit_grad = logit_grad.astype(BF)
    second_grad = gates[0] * routed[0][:, :width] + gates[1] * routed[1][:, :width]
    second_grad = second_grad + matmul(logit_grad, small_rows[:LANES])
    gain = small_rows[experts + 1 : experts + 2].astype(F32)
    first = high[:, :width]
    mixed_ref[...] = (first + gates[0] * returned[0] + gates[1] * returned[1]).astype(BF)
    inverse = inverse_rms(first)
    unit = first * inverse
    scaled = second_grad * gain
    first_grad = upstream + inverse * (
        scaled - unit * jnp.mean(unit * scaled, axis=-1, keepdims=True)
    )
    first_grad_ref[...] = first_grad
    first_low = first_grad.astype(BF)
    attended_grad = jnp.concatenate(
        [nt(first_low, part[:, part.shape[1] - width :]) for part in (near, far)], axis=1
    ).astype(BF)
    attended_grad = nt(attended_grad, shuffle).astype(BF)
    value_grad = []
    for number in range(width // LANES):
        outs = [
            tn(
                high[:, at_probs + head * count : at_probs + (head + 1) * count].astype(BF),
                pair_of(attended_grad, number),
            )
            for head in (2 * number, 2 * number + 1)
        ]
        value_grad.append(pick_heads(*outs).astype(BF))
    value_grad = jnp.concatenate(value_grad, axis=1)
    joint_grad_ref[:, 2 * width :] = value_grad
    gain_part = second_grad * unit
    gain_high = gain_part.astype(BF)
    gain_rest = (gain_part - gain_high.astype(F32)).astype(BF)
    ones = (lane == experts).astype(BF)
    left = jnp.concatenate([low[:, 5 * width :], gain_high, gain_rest], axis=0)
    left = matmul(left, shuffle).astype(BF)
    right = jnp.concatenate([logit_grad, ones, ones], axis=0)
    small = tn(left, right)
    row = lax.broadcasted_iota(jnp.int32, (count, count), 0)
    for number in range(width // LANES):
        span = slice(number * LANES, (number + 1) * LANES)
        query, keys, values = (
            low[:, i * width + number * LANES : i * width + (number + 1) * LANES] for i in range(3)
        )
        own_grad = attended_grad[:, span]
        query_grads, key_grads = [], []
        for side in range(2):
            head = 2 * number + side
            chance = high[:, at_probs + head * count : at_probs + (head + 1) * count]
            prob_grad = nt(one_head(own_grad, side), values)
            score_grad = chance * (prob_grad - jnp.sum(chance * prob_grad, axis=-1, keepdims=True))
            lined = score_grad
            step = 1
            while step < count:
                lined = jnp.where((row // step) % 2 == 1, pltpu.roll(lined, count - step, 1), lined)
                step *= 2
            distance_ref[head : head + 1] = jnp.sum(lined, axis=0, keepdims=True)
            pair_grad = (score_grad * 0.125).astype(BF)
            query_grads.append(matmul(pair_grad, keys))
            key_grads.append(tn(pair_grad, query))
        joint_grad_ref[:, span] = pick_heads(*query_grads).astype(BF)
        joint_grad_ref[:, width + number * LANES : width + (number + 1) * LANES] = pick_heads(
            *key_grads
        ).astype(BF)
    table = jnp.dot(
        distance_ref[...], flip_hot[...], precision=lax.Precision.HIGHEST, preferred_element_type=F32
    ).astype(BF)
    lanes = table_lanes(share)
    spread = keep_ref.shape[1] - 4 * width
    value_row = lax.broadcasted_iota(jnp.int32, (width, HEADS), 0) % share * lanes
    value_head = lax.broadcasted_iota(jnp.int32, (width, HEADS), 1)
    bucket = lax.broadcasted_iota(jnp.int32, (BUCKETS, spread), 0)
    lane = lax.broadcasted_iota(jnp.int32, (BUCKETS, spread), 1) - (experts + 1)
    small = jnp.pad(small, ((0, 0), (0, spread - LANES)))
    for start in range(0, max(lanes, BUCKETS), min(lanes, BUCKETS)):
        if lanes <= BUCKETS:
            picked = (value_row == value_head * BUCKETS + start).astype(BF)
            put = ((lane >= 0) & (lane < lanes) & (bucket == lane + start)).astype(BF)
        else:
            picked = (value_row + start == value_head * BUCKETS).astype(BF)
            put = (lane - start == bucket).astype(BF)
        small = small + matmul(picked, matmul(table, put).astype(BF))
    joint_grads = joint_grad_ref[...]
    for ref, at in ((keep_ref, 0), (send_ref, half)):
        attended, normed = (low[:, i * width + at : i * width + at + half] for i in (4, 3))
        ref[:, : 3 * width] = tn(normed, joint_grads).astype(BF)
        ref[:, 3 * width : 4 * width] = tn(attended, first_low).astype(BF)
        ref[:, 4 * width :] = small[at : at + half].astype(BF)


def token_kernel(
    experts,
    tokens,
    first_grad,
    joint_grad,
    near,
    far,
    place_of,
    token_ref,
    mark_ref,
):
    width = tokens.shape[1]
    shuffle = shuffle_of(place_of)
    gain = small_of(small_lanes(experts), near, far, shuffle)[experts : experts + 1].astype(F32)
    grads = joint_grad[...]
    normed_grad = jnp.concatenate(
        [nt(grads, part[:, : 3 * width]) for part in (near, far)], axis=1
    )
    large = normed_grad.astype(BF)
    rest = (normed_grad - large.astype(F32)).astype(BF)
    scaled = (nt(large, shuffle) + nt(rest, shuffle)) * gain
    inputs = tokens[...].astype(F32)
    inverse = inverse_rms(inputs)
    unit = inputs * inverse
    input_grad = inverse * (scaled - unit * jnp.mean(unit * scaled, axis=-1, keepdims=True))
    mark_ref[...] = jnp.zeros(mark_ref.shape, F32)
    token_ref[...] = (first_grad[...] + input_grad).astype(BF)


def finish_kernel(experts, leads, project_in, gain, *refs):
    parts, refs = refs[:-6], refs[-6:]
    grad_in_ref, sum_out_ref, router_ref, first_gain_ref, second_gain_ref, table_ref = refs
    sums = jnp.concatenate([sum_of(parts[:leads]), sum_of(parts[leads:])], axis=1)
    share, width = sum_out_ref.shape
    grad_in = sums[:, : 3 * width]
    grad_in_ref[...] = grad_in
    sum_out_ref[...] = sums[:, 3 * width : 4 * width]
    small = sums[:, 4 * width :]
    row = lax.broadcasted_iota(jnp.int32, (share, share), 0)
    same = row == lax.broadcasted_iota(jnp.int32, (share, share), 1)

    router_ref[...] = lax.dot_general(
        small[:, :experts],
        same.astype(F32),
        (((0,), (0,)), ((), ())),
        precision=lax.Precision.HIGHEST,
        preferred_element_type=F32,
    )

    def lined(column):
        return jnp.sum(jnp.where(same, column, 0.0), axis=0, keepdims=True)

    second_gain_ref[...] = lined(small[:, experts : experts + 1])
    grads = jnp.sum(grad_in * project_in[...].astype(F32), axis=-1, keepdims=True)
    first_gain_ref[...] = lined(grads) / gain[...].astype(F32)
    lanes = table_lanes(share)
    table = small[:, experts + 1 : experts + 1 + lanes]
    value_row = lax.broadcasted_iota(jnp.int32, (share, HEADS), 0) * lanes
    value_head = lax.broadcasted_iota(jnp.int32, (share, HEADS), 1)
    step = min(lanes, BUCKETS)
    total = jnp.zeros((HEADS, BUCKETS), F32)
    for start in range(0, max(lanes, BUCKETS), step):
        if lanes <= BUCKETS:
            picked, part = value_row == value_head * BUCKETS + start, table
        else:
            picked = value_row + start == value_head * BUCKETS
            part = table[:, start : start + step]
        put = lax.dot_general(
            picked.astype(F32),
            part,
            (((0,), (0,)), ((), ())),
            precision=lax.Precision.HIGHEST,
            preferred_element_type=F32,
        )
        if lanes <= BUCKETS:
            table_ref[:, start : start + step] = put
        else:
            total = total + put
            table_ref[...] = total


def on_device(
    tokens,
    cotangent,
    project_in,
    project_out,
    router,
    first_gain,
    second_gain,
    bias_table,
    expert_up,
    expert_down,
    positions,
    buckets,
    routes,
    slots,
):
    highest = lax.Precision.HIGHEST
    count, width = tokens.shape
    experts = lax.axis_size("expert")
    capacity = 3 * count // experts
    rows_here = experts * capacity
    share = project_in.shape[0]
    column = lax.axis_index("fsdp")
    mine = column * experts + lax.axis_index("expert")
    target = routes * capacity + slots
    slot_index = jnp.arange(rows_here, dtype=jnp.int32)
    hot = (slot_index[None, None, :] == jnp.transpose(target)[:, :, None]).astype(BF)
    place_hot = hot[0] + hot[1]
    grad_rows = contract_rows(place_hot, cotangent).astype(BF)
    grad_own = exchange(grad_rows)

    lanes = small_lanes(experts)
    hidden = expert_down.shape[1]
    late = hidden - hidden // 2 // LANES * LANES
    packed, down_own = kernel_call(
        pack_kernel,
        [((share, lanes + 4 * width), BF), ((hidden - late, width), BF)],
        0,
        router.T,
        first_gain[None],
        second_gain[None],
        project_in,
        project_out,
        expert_down,
        fetch=(*range(5), (5, (0, slice(late, hidden)), (hidden - late, width))),
        scratch=56,
    )
    weights = stack([expert_up[0].T, expert_down[0, :late]])
    downs = fan(down_own, chip_masks())
    halves = gather_blocks(packed, (weights, *downs[1:]), (grad_own,))
    grad_parts = (grad_own, swap(grad_own, core_mask()))
    weights = fan(after(weights, halves[0]), chip_masks())
    feature = jnp.arange(width, dtype=jnp.int32)
    masks = jnp.asarray(np.repeat(np.array(block_masks(), np.int32), share))
    place_of = (masks ^ mine) * share + feature % share


    places = jnp.arange(count, dtype=jnp.int32)
    bucket_hot = (buckets[:, None] == jnp.arange(BUCKETS, dtype=jnp.int32)).astype(F32)
    flip = ((places[:, None] + places[None, :]) % count == 0).astype(F32)
    flip_hot = jnp.dot(flip, bucket_hot, precision=highest)
    bias_rows = lax.dot_general(
        bias_table, flip_hot, (((0,), (1,)), ((), ())), precision=highest
    )
    low, high, outgoing = kernel_call(
        functools.partial(forward_kernel, experts),
        [
            ((count, 6 * width), BF),
            ((count, width + LANES + HEADS * count), F32),
            ((rows_here, width + LANES), BF),
        ],
        2 * count * width * 6 * width,
        tokens,
        place_of[None],
        *halves,
        bias_rows,
        positions[:, None],
        routes,
        jnp.transpose(target),
        fetch=(0, 2, 3, 1, 4, 5, 6, 7),
        push=(0, 1, 2),
        scratch=56,
    )
    row_own = exchange(outgoing)
    row_parts = (row_own, swap(row_own, core_mask()))

    chips = len(chip_masks())
    piece = expert_up.shape[2]
    wide = (rows_here, 2 * width)
    row_far, row_near, kept, shown = kernel_call(
        functools.partial(expert_kernel, chips),
        [
            (wide, BF),
            (wide, BF),
            ((2 * rows_here, 2 * piece + width), BF),
            ((2 * rows_here, width), BF),
        ],
        16 * rows_here * width * chips * piece,
        row_parts[1],
        row_parts[0],
        grad_parts[1],
        grad_parts[0],
        *weights,
        *downs,
        fetch=range(4, 4 + 2 * chips),
        scratch=50,
    )
    others = [swap(shown, mask) for mask in chip_masks()[1:]]
    others = [both for part in others for both in (part, swap(part, core_mask()))]
    (row_sum,) = sum_apart([row_near, swap(row_far, core_mask())], 1)
    home = after(exchange(row_sum), *others)

    half = width // 2
    table_at = experts + 1
    spread_lanes = -(-(table_at + table_lanes(share)) // LANES) * LANES
    keep, send, first_grad, joint_grad, _, mixed = kernel_call(
        functools.partial(home_kernel, experts, share),
        [
            ((half, 4 * width + spread_lanes), BF),
            ((half, 4 * width + spread_lanes), BF),
            ((count, width), F32),
            ((count, 3 * width), BF),
            ((HEADS, count), F32),
            ((count, width), BF),
        ],
        2 * count * width * 10 * width,
        home,
        routes,
        target,
        cotangent,
        place_of[None],
        low,
        high,
        *halves,
        flip_hot,
        fetch=(
            6,
            (7, (slice(None), slice(3 * width, None)), (half, lanes + width)),
            (8, (slice(None), slice(3 * width, None)), (half, lanes + width)),
            3,
            5,
        ),
        scratch=50,
    )
    def token_parts(begun):
        return kernel_call(
            functools.partial(token_kernel, experts),
            [((count, width), BF), ((8, LANES), F32)],
            2 * count * width * 6 * width,
            tokens,
            first_grad,
            joint_grad,
            *halves,
            place_of[None],
            fetch=(3, 4, 0, 1, 2),
            near=(begun,),
            scratch=56,
        )

    def weight_parts(begun):
        return kernel_call(
            weight_grad_kernel,
            [((width, piece), F32), ((piece, width), F32), ((8, LANES), F32)],
            16 * rows_here * width * chips * piece,
            weights[0],
            down_own,
            kept,
            row_parts[1],
            row_parts[0],
            *others,
            fetch=range(5 + len(others)),
            near=(begun,),
            scratch=56,
        )

    leads, trails, (grad_up, grad_down, _), (token_grad, mark) = scatter_blocks(
        keep, send, weight_parts, token_parts
    )
    grad_in, sum_out, grad_router, grad_first_gain, grad_second_gain, table_total = kernel_call(
        functools.partial(finish_kernel, experts, len(leads)),
        [
            ((share, 3 * width), F32),
            ((share, width), F32),
            ((experts, share), F32),
            ((1, share), F32),
            ((1, share), F32),
            ((HEADS, BUCKETS), F32),
        ],
        share * width * 8,
        project_in,
        first_gain[None],
        *leads,
        *trails,
        near=(mark,),
    )
    return (
        mixed,
        token_grad,
        grad_in,
        sum_out,
        grad_router.T,
        grad_first_gain[0],
        grad_second_gain[0],
        table_total.T,
        grad_up[None],
        grad_down[None],
    )


def solution(mesh):
    rows = P(("fsdp", "expert"), None)
    line = P(("fsdp", "expert"))
    up, down = P("expert", None, "fsdp"), P("expert", "fsdp", None)
    return jax.shard_map(
        on_device,
        mesh=mesh,
        in_specs=(rows, rows, rows, rows, rows, line, line, P(), up, down, line, P(), rows, rows),
        out_specs=(rows, rows, rows, rows, rows, line, line, P(), up, down),
        check_vma=False,
    )
```
